256 devices in a mesh: grp: 2 (over core), fsdp: 16 (over z_lo, x), seq: 8 (over z_hi, y).
Axes of the slice: x: 4, y: 4, z: 8 (z_hi: 2, z_lo: 4; z = z_hi * 4 + z_lo), core: 2. Of those that a mesh axis runs over, the one named last changes fastest.
Arguments:
- clip_input: bfloat16 [32, 1024, 3072], P(('grp', 'fsdp'), 'seq'), may hold values from -6 to 6
- qkv_input: bfloat16 [32, 1024, 6144], P(('grp', 'fsdp'), 'seq'), may hold values from -12 to 12
- prompt_states: bfloat16 [32, 512, 4096], P(('grp', 'fsdp'), 'seq'), may hold values from -6 to 6
- prompt_ids: int32 [32, 512], P(('grp', 'fsdp'), 'seq'), may hold values from 0 to 32127, as said below
- t5_gain: float32 [4096], replicated, may hold values from 0.1 to 1.9
- w_text: bfloat16 [4096, 4096], P('seq', ('grp', 'fsdp')), may hold values from -0.09375 to 0.09375
- w_out: bfloat16 [2048, 3072], P('seq', ('grp', 'fsdp')), may hold values from -0.125 to 0.125
- gate_table: bfloat16 [1000, 3072], replicated, may hold values from -6 to 6
- timesteps: int32 [32], P(('grp', 'fsdp')), may hold values from 0 to 999
- out_cotangent: bfloat16 [32, 1024, 3072], P(('grp', 'fsdp'), 'seq'), may hold values from -6 to 6
Outputs:
- block_out: bfloat16 [32, 1024, 3072], P(('grp', 'fsdp'), 'seq')
- qkv_grad: bfloat16 [32, 1024, 6144], P(('grp', 'fsdp'), 'seq')
- w_out_grad: float32 [2048, 3072], P('seq', ('grp', 'fsdp'))
The draws below stay inside these ranges and needn't reach their ends.
Inputs may be any that keep to these rules, and one draw needn't show every extreme that they name: `prompt_ids`: each prompt is a run of ids from 1 to 32127 of 128 to 512 tokens followed by zeros; some prompt has no zeros.
All inputs are finite; a program needn't handle non-finite values.
Results may differ from the reference program's by a relative error of at most 0.03.
Values may be sent and summed in bfloat16 or wider, within the bound.
A program may use at most 128 MiB of HBM per device.

```python
import math
import jax
import jax.numpy as jnp
from jax import lax

D = 3072
H = 16
HD = 128
DT = 4096
P_SIZE = 512
VOCAB = 32128
STEPS = 1000
LEN = 1024
CLIPS = 32
HH = 2048
N_SEQ = 8


def draw_qkv_input(key, part):
    key = jax.random.fold_in(key, 11)
    drawn = jax.random.normal(key, (CLIPS, LEN, H, 3, HD), jnp.float32)
    spread = jnp.array([2.5, 1.0, 1.0], jnp.float32)[:, None]
    drawn = jnp.clip(drawn * spread, -12.0, 12.0)
    return drawn.reshape(CLIPS, LEN, H * 3 * HD).astype(jnp.bfloat16)


def draw_prompt_ids(key, part):
    key = jax.random.fold_in(key, 23)
    live_len = jax.random.randint(jax.random.fold_in(key, 1), (CLIPS,), P_SIZE // 4, P_SIZE + 1)
    clip_index = jnp.arange(CLIPS)
    live_len = jnp.where(clip_index == 0, P_SIZE, jnp.where(clip_index == 1, P_SIZE // 4, live_len))
    tokens_drawn = jax.random.randint(jax.random.fold_in(key, 2), (CLIPS, P_SIZE), 1, VOCAB)
    top_slot = (clip_index[:, None] == 0) & (jnp.arange(P_SIZE)[None, :] == 0)
    tokens_drawn = jnp.where(top_slot, VOCAB - 1, tokens_drawn)
    return jnp.where(jnp.arange(P_SIZE)[None, :] < live_len[:, None], tokens_drawn, 0).astype(jnp.int32)


def plant(result, rng, low, high):
    extent = result.shape
    spot = [jax.random.randint(jax.random.fold_in(rng, axis), (), 0, extent[axis]) for axis in range(len(extent))]
    result = result.at[tuple(spot)].set(low)
    longest = extent.index(max(extent))
    spot[longest] = (spot[longest] + 1) % extent[longest]
    return result.at[tuple(spot)].set(high)


def steps_of(own_key, shape, pieces, least, high):
    def one(dim, shards_of):
        heights = jax.random.uniform(jax.random.fold_in(jax.random.fold_in(own_key, 6), dim), (shards_of,), jnp.float32, least / len(pieces), high / len(pieces))
        return jnp.repeat(jnp.exp(heights), shape[dim] // shards_of).reshape((-1,) + (1,) * (len(shape) - dim - 1))

    loudness = one(*pieces[0])
    for cut in pieces[1:]:
        loudness = loudness * one(*cut)
    return loudness


def gaussian(own_key, shape, scale, limit, split=(), held_as=jnp.bfloat16):
    gain = steps_of(own_key, shape, split, -0.22, 0.18) if split else 1.0
    values = jax.random.normal(own_key, shape, jnp.float32) * scale * gain
    return jnp.minimum(jnp.maximum(values, -limit), limit).astype(held_as)


def setup_inputs(seed: int = 0) -> dict:
    streams_of = jax.random.split(jax.random.key(seed), 11)
    clip_input = gaussian(streams_of[0], (CLIPS, LEN, D), 1.0, 6.0, ((0, 32), (1, 8)))
    qkv_input = draw_qkv_input(jax.random.fold_in(streams_of[10], 71), 0)
    prompt_states = gaussian(streams_of[2], (CLIPS, P_SIZE, DT), 1.0, 6.0, ((0, 32), (1, 8)))
    prompt_ids = draw_prompt_ids(jax.random.fold_in(streams_of[10], 71), 0)
    t5_gain = jnp.clip(1.0 + 0.18 * jax.random.normal(streams_of[4], (DT,), jnp.float32), 0.1, 1.9)
    w_text = gaussian(streams_of[5], (2 * HH, DT), DT ** -0.5, 0.09375, ((0, 8), (1, 32)))
    w_out = gaussian(streams_of[6], (HH, D), HH ** -0.5, 0.125, ((0, 8), (1, 32)))
    gate_table = gaussian(streams_of[7], (STEPS, D), 1.5, 6.0)
    timesteps = plant(jax.random.randint(streams_of[8], (CLIPS,), 0, STEPS), jax.random.fold_in(streams_of[8], 1), 0, STEPS - 1).astype(jnp.int32)
    out_cotangent = gaussian(streams_of[9], (CLIPS, LEN, D), 1.0, 6.0, ((0, 32), (1, 8)))
    return dict(clip_input=clip_input, qkv_input=qkv_input, prompt_states=prompt_states, prompt_ids=prompt_ids, t5_gain=t5_gain, w_text=w_text, w_out=w_out, gate_table=gate_table, timesteps=timesteps, out_cotangent=out_cotangent)


norm_eps = 1e-06
masked_score = -1e+30

def score_block(query_block, key_rows, key_live, score_scale):
    scores = jnp.einsum('bge,kge->gbk', query_block.astype(jnp.float32), key_rows.astype(jnp.float32)) * score_scale
    scores = jnp.where(key_live[None, None, :], scores, masked_score)
    row_peak = lax.optimization_barrier(jnp.max(scores, axis=-1, keepdims=True))
    shifted = jnp.exp(scores - row_peak)
    return shifted / lax.optimization_barrier(jnp.sum(shifted, axis=-1, keepdims=True))

def attend_forward(queries, key_rows, value_rows, key_live, score_scale):
    length = queries.shape[0]
    block_rows = min(512, length)
    query_blocks = queries.reshape((length // block_rows, block_rows) + queries.shape[1:])

    def one_block(query_block):
        soft_half = score_block(query_block, key_rows, key_live, score_scale).astype(jnp.bfloat16)
        return jnp.einsum('gbk,kge->bge', soft_half.astype(jnp.float32), value_rows.astype(jnp.float32)).astype(jnp.bfloat16)
    return lax.map(one_block, query_blocks).reshape(queries.shape)

def attend_backward(queries, key_rows, value_rows, key_live, score_scale, attended, out_grad):
    length = queries.shape[0]
    block_rows = min(512, length)
    block_total = length // block_rows
    query_blocks = queries.reshape((block_total, block_rows) + queries.shape[1:])
    attended_blocks = attended.reshape((block_total, block_rows) + attended.shape[1:])
    grad_blocks = out_grad.reshape((block_total, block_rows) + out_grad.shape[1:])

    def one_block(carried, inputs):
        key_acc, value_acc = carried
        query_block, attended_block, grad_block = inputs
        soft_rows = score_block(query_block, key_rows, key_live, score_scale)
        soft_half = soft_rows.astype(jnp.bfloat16)
        grad_soft = jnp.einsum('bge,kge->gbk', grad_block.astype(jnp.float32), value_rows.astype(jnp.float32))
        row_dot = lax.optimization_barrier(jnp.sum(grad_block.astype(jnp.float32) * attended_block.astype(jnp.float32), axis=-1))
        grad_score = (soft_rows * (grad_soft - jnp.transpose(row_dot)[:, :, None]) * score_scale).astype(jnp.bfloat16)
        query_grad = jnp.einsum('gbk,kge->bge', grad_score.astype(jnp.float32), key_rows.astype(jnp.float32)).astype(jnp.bfloat16)
        key_acc = key_acc + jnp.einsum('gbk,bge->kge', grad_score.astype(jnp.float32), query_block.astype(jnp.float32))
        value_acc = value_acc + jnp.einsum('gbk,bge->kge', soft_half.astype(jnp.float32), grad_block.astype(jnp.float32))
        return ((key_acc, value_acc), query_grad)
    zeros_acc = jnp.zeros(key_rows.shape, jnp.float32)
    (key_acc, value_acc), query_grads = lax.scan(one_block, (zeros_acc, zeros_acc), (query_blocks, attended_blocks, grad_blocks))
    return (query_grads.reshape(queries.shape), key_acc[:length].astype(jnp.bfloat16), value_acc[:length].astype(jnp.bfloat16))

def reference(clip_input, qkv_input, prompt_states, prompt_ids, t5_gain, w_text, w_out, gate_table, timesteps, out_cotangent):
    score_scale = 1.0 / math.sqrt(HD)
    group_rows = H * HD // N_SEQ

    def one_clip(weight_sum, inputs):
        clip_rows, qkv_rows, states, ids_row, step_index, cotangent = inputs
        wide_states = states.astype(jnp.float32)
        normed = (wide_states * lax.rsqrt(lax.optimization_barrier(jnp.mean(wide_states * wide_states, axis=-1, keepdims=True)) + norm_eps) * t5_gain).astype(jnp.bfloat16)
        text_kv = jnp.dot(normed, w_text.T, preferred_element_type=jnp.float32).astype(jnp.bfloat16).reshape(P_SIZE, H, 2 * HD)
        head_rows = qkv_rows.reshape(LEN, H, 3 * HD)
        queries = head_rows[:, :, :HD]
        key_rows = jnp.concatenate([head_rows[:, :, HD:2 * HD], text_kv[:, :, :HD]], axis=0)
        value_rows = jnp.concatenate([head_rows[:, :, 2 * HD:], text_kv[:, :, HD:]], axis=0)
        key_live = jnp.concatenate([jnp.ones((LEN,), bool), ids_row != 0])
        attended = attend_forward(queries, key_rows, value_rows, key_live, score_scale)
        attended_flat = attended.reshape(LEN, H * HD)
        group_parts = jnp.einsum('lnr,nrd->nld', attended_flat.reshape(LEN, N_SEQ, group_rows).astype(jnp.float32), w_out.reshape(N_SEQ, group_rows, D).astype(jnp.float32))
        group_parts = lax.optimization_barrier(group_parts.astype(jnp.bfloat16)).astype(jnp.float32)
        projected = lax.optimization_barrier(jnp.sum(group_parts, axis=0))
        gate_row = lax.dynamic_index_in_dim(gate_table, step_index, 0, keepdims=False).astype(jnp.float32)
        block_mixed = (clip_rows.astype(jnp.float32) + gate_row * projected).astype(jnp.bfloat16)
        proj_grad = (gate_row * cotangent.astype(jnp.float32)).astype(jnp.bfloat16)
        attended_grad = jnp.dot(proj_grad, w_out.T, preferred_element_type=jnp.float32).astype(jnp.bfloat16).reshape(LEN, H, HD)
        weight_sum = weight_sum + jnp.dot(attended_flat.T, proj_grad, preferred_element_type=jnp.float32)
        query_grad, key_grad, value_grad = attend_backward(queries, key_rows, value_rows, key_live, score_scale, attended, attended_grad)
        qkv_rows_grad = jnp.concatenate([query_grad, key_grad, value_grad], axis=2).reshape(LEN, H * 3 * HD)
        return (weight_sum, (block_mixed, qkv_rows_grad))
    weight_sum, (block_out, qkv_grad) = lax.scan(one_clip, jnp.zeros((H * HD, D), jnp.float32), (clip_input, qkv_input, prompt_states, prompt_ids, timesteps, out_cotangent))
    return (block_out, qkv_grad, weight_sum)
```

```python
import functools
import math

import jax
import jax.numpy as jnp
from jax import lax
from jax.experimental import pallas as pl
from jax.experimental.pallas import tpu as pltpu
from jax.sharding import PartitionSpec as P

H = 16
HD = 128
D = 3072
DT = 4096
LEN = 1024
PROMPT = 512
TOK = 128
PTOK = 64
HALF = 512
PHALF = 256
FEAT = 256
COLS = 96
QB = 256

MESH = pl.DeviceIdType.MESH
BF = jnp.bfloat16
F32 = jnp.float32

norm_eps = 1e-06
masked_score = -1e30
score_scale = 1.0 / math.sqrt(HD)
log2e = math.log2(math.e)

N_COPIES = 140


def nt(a, b):
    return lax.dot_general(a, b, (((1,), (1,)), ((), ())), preferred_element_type=F32)


def nn(a, b):
    return lax.dot_general(a, b, (((1,), (0,)), ((), ())), preferred_element_type=F32)


def body(
    gate, gain, cot, clip, prm, ids, wtin, woin, qkv,
    bo, dqo, wgo,
    wt, wo, pg, pgt, nrm, cnts, qkvs, dos, dosend, tkv, tksend,
    kb, vb, kt, vt, dka, dva, att, aabs, dqs,
    psend, pown, precv, wsend, wrecv, wown, wxs, wxr, wzs, wzr,
    send_sem, recv_sem, loc_sem,
):
    g = lax.axis_index("grp")
    f = lax.axis_index("fsdp")
    s = lax.axis_index("seq")
    zlo, x = lax.div(f, 4), lax.rem(f, 4)
    zhi, y = lax.div(s, 4), lax.rem(s, 4)
    z = zhi * 4 + zlo
    ozhi = 1 - zhi

    def at(gg, xx, yy, zz):
        return (gg, lax.rem(zz, 4) * 4 + xx, lax.div(zz, 4) * 4 + yy)

    sib = at(1 - g, x, y, z)
    xd = [at(g, lax.rem(x + j, 4), y, z) for j in range(4)]
    yd = [at(g, x, lax.rem(y + j, 4), z) for j in range(4)]
    zd = [at(g, x, y, lax.rem(z + j, 8)) for j in range(8)]
    clip_peers = []
    for dz in range(2):
        for dy in range(4):
            if dz or dy:
                py, pz = lax.rem(y + dy, 4), lax.rem(z + 4 * dz, 8)
                clip_peers.append((at(g, x, py, pz), lax.div(pz, 4) * 4 + py))
    partner = zd[4]
    peers = [sib] + xd[1:] + zd[1:] + [clip_peers[i][0] for i in (0, 1, 2, 4, 5, 6)]

    barrier = pltpu.get_barrier_semaphore()
    for p in peers:
        pl.semaphore_signal(barrier, inc=1, device_id=p, device_id_type=MESH)

    started = []

    def send(src, dst, device):
        i = len(started)
        c = pltpu.make_async_remote_copy(
            src_ref=src, dst_ref=dst, send_sem=send_sem.at[i], recv_sem=recv_sem.at[i],
            device_id=device, device_id_type=MESH,
        )
        c.start()
        started.append(c)
        return c

    def slot(zz):
        d = lax.rem(zz - z + 8, 8)
        return jnp.minimum(2 * d, 15 - 2 * d)

    wo[g, x, 0] = woin[...]
    wt[g, x, 0] = wtin[...]
    gate_row = gate[...].astype(F32)
    my_rows = pl.ds(pl.multiple_of(y * TOK, TOK), TOK)
    pg[my_rows, :] = (gate_row * cot[...].astype(F32)).astype(BF)
    my_prompt = pl.ds(pl.multiple_of(y * PTOK, PTOK), PTOK)
    wide = prm[...].astype(F32)
    mean = jnp.mean(wide * wide, axis=-1, keepdims=True)
    nrm[my_prompt, :] = (wide * lax.rsqrt(mean + norm_eps) * gain[...]).astype(BF)
    live = jnp.sum((ids[...] != 0).astype(jnp.int32), axis=-1, keepdims=True)
    cnts[0] = jnp.broadcast_to(live, (8, 128))

    pl.semaphore_wait(barrier, len(peers))

    def zstep(buf, k):
        if k < 4:
            a, b = (0, 0) if k == 1 else (2 * k - 3, 2 * k - 2)
            return [
                send(buf.at[g, x, a], buf.at[g, x, 2 * k - 1], zd[1]),
                send(buf.at[g, x, b], buf.at[g, x, 2 * k], zd[7]),
            ]
        h = buf.shape[3] // 2
        top, bottom = pl.ds(0, h), pl.ds(h, h)
        return [
            send(buf.at[g, x, 5, top], buf.at[g, x, 7, top], zd[1]),
            send(buf.at[g, x, 6, bottom], buf.at[g, x, 7, bottom], zd[7]),
        ]

    groups = ((0, 1), (1, 2), (3, 2), (5, 2), (7, 1))

    def xfirst(buf, k):
        sl = pl.ds(*groups[k])
        mine = buf.at[g, x, sl]
        return [send(mine, mine, xd[1]), send(mine, mine, xd[3])]

    def xsecond(buf, k):
        first, n = groups[k]
        lx, rx = lax.rem(x + 3, 4), lax.rem(x + 1, 4)
        if n == 2:
            from_left, from_right = buf.at[g, lx, first], buf.at[g, rx, first + 1]
        else:
            h = buf.shape[3] // 2
            from_left = buf.at[g, lx, first, pl.ds(0, h)]
            from_right = buf.at[g, rx, first, pl.ds(h, h)]
        return [send(from_left, from_left, xd[1]), send(from_right, from_right, xd[3])]

    def to_sibling(buf, k):
        both = buf.at[g, :, pl.ds(*groups[k])]
        return [send(both, both, sib)]

    def got(copies):
        for c in copies:
            c.wait_recv()

    def yfirst(buf, n):
        mine = buf.at[pl.ds(pl.multiple_of(y * n, n), n), :]
        return [send(mine, mine, yd[1]), send(mine, mine, yd[3])]

    def ysecond(buf, n):
        h = n // 2
        from_left = buf.at[pl.ds(pl.multiple_of(lax.rem(y + 3, 4) * n, n), h), :]
        from_right = buf.at[pl.ds(pl.multiple_of(lax.rem(y + 1, 4) * n + h, h), h), :]
        return [send(from_left, from_left, yd[1]), send(from_right, from_right, yd[3])]

    zo, zt, xo, xt, xo2, xt2, so, st = {}, {}, {}, {}, {}, {}, {}, {}
    zo[1] = zstep(wo, 1)
    zt[1] = zstep(wt, 1)
    xo[0] = xfirst(wo, 0)
    xt[0] = xfirst(wt, 0)
    pg1 = yfirst(pg, TOK)
    n1 = yfirst(nrm, PTOK)
    cnt_copies = [
        send(cnts.at[0], cnts.at[i + 1], dev) for i, (dev, _) in enumerate(clip_peers)
    ]
    qkv_copies = []
    my_token_rows = pl.ds(pl.multiple_of(s * TOK, TOK), TOK)
    for dev, ps in reversed(clip_peers):
        qkv_copies.append(
            send(qkv.at[:, pl.ds(pl.multiple_of(ps * 768, 768), 768)], qkvs.at[my_token_rows, :], dev)
        )
    own_qkv = pltpu.make_async_copy(
        qkv.at[:, pl.ds(pl.multiple_of(s * 768, 768), 768)], qkvs.at[my_token_rows, :], loc_sem.at[0]
    )
    own_qkv.start()

    for k in range(1, 5):
        got(zo[k])
        if k < 4:
            zo[k + 1] = zstep(wo, k + 1)
        xo[k] = xfirst(wo, k)
        got(zt[k])
        if k < 4:
            zt[k + 1] = zstep(wt, k + 1)
        xt[k] = xfirst(wt, k)
        got(xo[k - 1])
        xo2[k - 1] = xsecond(wo, k - 1)
        got(xt[k - 1])
        xt2[k - 1] = xsecond(wt, k - 1)
        if k >= 2:
            got(xo2[k - 2])
            so[k - 2] = to_sibling(wo, k - 2)
            got(xt2[k - 2])
            st[k - 2] = to_sibling(wt, k - 2)
        if k == 2:
            got(pg1)
            pg2 = ysecond(pg, TOK)
        if k == 3:
            got(n1)
            n2 = ysecond(nrm, PTOK)
    got(xo[4])
    xo2[4] = xsecond(wo, 4)
    got(xt[4])
    xt2[4] = xsecond(wt, 4)
    for k in (3, 4):
        got(xo2[k])
        so[k] = to_sibling(wo, k)
    got(pg2)
    for k in range(5):
        got(so[k])

    def attended_grad(zh, dst, row0):
        def rows(i, carry):
            acc = jnp.zeros((TOK, FEAT), F32)
            here = pl.ds(pl.multiple_of(i * TOK, TOK), TOK)
            for gg in range(2):
                for q in range(4):
                    w = wo[gg, :, slot(zh * 4 + q)].reshape(4 * COLS, FEAT)
                    acc += nn(pg[here, pl.ds((gg * 4 + q) * 384, 384)], w)
            dst[pl.ds(pl.multiple_of(row0 + i * TOK, TOK), TOK), :] = acc.astype(BF)
            return carry

        lax.fori_loop(0, HALF // TOK, rows, 0)

    attended_grad(ozhi, dosend, 0)
    half_rows = pl.ds(pl.multiple_of(zhi * HALF, HALF), HALF)
    do_copy = send(dosend, dos.at[half_rows, :], partner)
    attended_grad(zhi, dos, zhi * HALF)

    def turn(i, carry):
        c = pl.ds(pl.multiple_of(i * 128, 128), 128)
        pgt[c, :] = pg[:, c].T
        return carry

    lax.fori_loop(0, D // 128, turn, 0)

    for k in (3, 4):
        got(xt2[k])
        st[k] = to_sibling(wt, k)
    got(n2)
    for k in range(5):
        got(st[k])

    def prompt_kv(zh, dst, row0):
        def rows(i, carry):
            acc = jnp.zeros((128, 512), F32)
            here = pl.ds(pl.multiple_of(i * 128, 128), 128)
            for gg in range(2):
                for q in range(4):
                    sl = slot(zh * 4 + q)
                    w = jnp.concatenate([wt[gg, xx, sl] for xx in range(4)], axis=1)
                    acc += nt(nrm[here, pl.ds((gg * 4 + q) * 512, 512)], w)
            dst[pl.ds(pl.multiple_of(row0 + i * 128, 128), 128), :] = acc.astype(BF)
            return carry

        lax.fori_loop(0, PHALF // 128, rows, 0)

    prompt_kv(ozhi, tksend, 0)
    tk_copy = send(tksend, tkv.at[pl.ds(pl.multiple_of(zhi * PHALF, PHALF), PHALF), :], partner)
    prompt_kv(zhi, tkv, zhi * PHALF)

    got(cnt_copies)
    total = cnts[0]
    for i in range(1, 8):
        total += cnts[i]
    live_row = total[0:1, 0:1]
    own_qkv.wait()
    got(qkv_copies)
    do_copy.wait_recv()
    tk_copy.wait_recv()

    def heads(h):
        kb[pl.ds(0, LEN), :] = qkvs[:, pl.ds(h * 384 + 128, 128)]
        vb[pl.ds(0, LEN), :] = qkvs[:, pl.ds(h * 384 + 256, 128)]
        kb[pl.ds(LEN, PROMPT), :] = tkv[:, pl.ds(h * 256, 128)]
        vb[pl.ds(LEN, PROMPT), :] = tkv[:, pl.ds(h * 256 + 128, 128)]
        kt[...] = kb[...].T
        vt[...] = vb[...].T
        dka[...] = jnp.zeros_like(dka)
        dva[...] = jnp.zeros_like(dva)

        def block(i, carry):
            here = pl.ds(pl.multiple_of(i * QB, QB), QB)
            q = qkvs[here, pl.ds(h * 384, 128)]
            do = dos[here, pl.ds(h * 128, 128)]
            t = nt(kb[...], q) * (score_scale * log2e)
            row = lax.broadcasted_iota(jnp.int32, (PROMPT, QB), 0)
            t_prompt = jnp.where(row < live_row, t[LEN:], masked_score)
            t = jnp.concatenate([t[:LEN], t_prompt], axis=0)
            e = jnp.exp2(t - jnp.max(t, axis=0, keepdims=True))
            p = e * (1.0 / jnp.sum(e, axis=0, keepdims=True))
            pb = p.astype(BF)
            o_t = nn(vt[...], pb).astype(BF).astype(F32)
            att[here, pl.ds(h * 128, 128)] = o_t.T.astype(BF)
            row_dot = jnp.sum(do.astype(F32).T * o_t, axis=0, keepdims=True)
            dp = nt(vb[...], do)
            ds = (p * (dp - row_dot)).astype(BF)
            dq_t = nn(kt[...], ds) * score_scale
            dqs[here, pl.ds(h * 384, 128)] = dq_t.T.astype(BF)
            dka[...] += nn(ds[:LEN], q)
            dva[...] += nn(pb[:LEN], do)
            return carry

        lax.fori_loop(0, LEN // QB, block, 0)
        dqs[:, pl.ds(h * 384 + 128, 128)] = (dka[...] * score_scale).astype(BF)
        dqs[:, pl.ds(h * 384 + 256, 128)] = dva[...].astype(BF)

    att_copies, dq_copies = [], []
    for h in range(2):
        heads(h)
        hl = pl.ds(h * 128, 128)
        theirs = pl.ds(pl.multiple_of(ozhi * HALF, HALF), HALF)
        att_copies.append(send(att.at[theirs, hl], aabs.at[zhi, :, hl], partner))
        hq = pl.ds(h * 384, 384)
        out_cols = pl.ds(pl.multiple_of(s * 768 + h * 384, 384), 384)
        for dev, ps in reversed(clip_peers):
            rows = pl.ds(pl.multiple_of(ps * TOK, TOK), TOK)
            dq_copies.append(send(dqs.at[rows, hq], dqo.at[:, out_cols], dev))
        dqo[:, out_cols] = dqs[my_token_rows, hq]
        aabs[zhi, :, hl] = att[half_rows, hl]

    got(att_copies)

    def project(rows, put):
        for gg in range(2):
            for q in range(4):
                acc = None
                for zh in range(2):
                    w = wo[gg, :, slot(zh * 4 + q)].reshape(4 * COLS, FEAT)
                    term = nt(aabs[zh, rows, :], w)
                    acc = term if acc is None else acc + term
                put(pl.ds((gg * 4 + q) * 384, 384), acc)

    p_copies = []
    for j in (2, 1, 3):
        rows = pl.ds(pl.multiple_of(lax.rem(y + j, 4) * TOK, TOK), TOK)

        def put_send(c, v, j=j):
            psend[j - 1, :, c] = v.astype(BF)

        project(rows, put_send)
        p_copies.append(send(psend.at[j - 1], precv.at[j - 1], yd[j]))

    def weight_grad(gg, dst, dtype):
        def group(q, carry):
            rows = pl.ds(pl.multiple_of((gg * 4 + q) * 384, 384), 384)
            for zh in range(2):
                w = nn(pgt[rows, :], aabs[zh])
                dst[:, zh * 4 + q] = w.reshape(4, COLS, FEAT).astype(dtype)
            return carry

        lax.fori_loop(0, 4, group, 0)

    weight_grad(1 - g, wsend, BF)
    w_copy = send(wsend, wrecv, sib)
    weight_grad(g, wown, F32)

    def put_own(c, v):
        pown[:, c] = v

    project(my_rows, put_own)

    w_copy.wait_recv()

    def chip_sum(i, carry):
        xx, zz = lax.div(i, 8), lax.rem(i, 8)
        wxs[xx, zz] = (wown[xx, zz] + wrecv[xx, zz].astype(F32)).astype(BF)
        return carry

    lax.fori_loop(0, 32, chip_sum, 0)
    wx_copies = [send(wxs.at[lax.rem(x + j, 4)], wxr.at[j - 1], xd[j]) for j in (2, 1, 3)]

    got(wx_copies)

    def x_sum(i, carry):
        v = wxs[x, i].astype(F32)
        for j in range(3):
            v += wxr[j, i].astype(F32)
        wzs[i] = v.astype(BF)
        return carry

    lax.fori_loop(0, 8, x_sum, 0)
    wz_copies = [send(wzs.at[lax.rem(z + j, 8)], wzr.at[j - 1], zd[j]) for j in (4, 3, 5, 2, 6, 1, 7)]

    got(p_copies)
    proj = pown[...]
    for j in range(3):
        proj += precv[j].astype(F32)
    bo[...] = (clip[...].astype(F32) + gate_row * proj).astype(BF)

    got(wz_copies)
    v = wzs[z].astype(F32)
    for j in range(7):
        v += wzr[j].astype(F32)
    wgo[...] = v

    got(dq_copies)
    for c in started:
        c.wait_send()


def per_device(
    clip_input, qkv_input, prompt_states, prompt_ids, t5_gain, w_text, w_out, gate_table,
    timesteps, out_cotangent,
):
    gate_row = lax.dynamic_index_in_dim(gate_table, timesteps[0], 0, keepdims=True)
    vmem = pl.BlockSpec(memory_space=pltpu.VMEM)
    anym = pl.BlockSpec(memory_space=pl.ANY)
    vm = pltpu.VMEM
    scratch = [
        vm((2, 4, 8, 512, 128), BF),
        vm((2, 4, 8, COLS, FEAT), BF),
        vm((HALF, D), BF),
        vm((D, HALF), BF),
        vm((PHALF, DT), BF),
        vm((8, 8, 128), jnp.int32),
        vm((LEN, 768), BF),
        vm((LEN, FEAT), BF),
        vm((HALF, FEAT), BF),
        vm((PROMPT, 512), BF),
        vm((PHALF, 512), BF),
        vm((LEN + PROMPT, HD), BF),
        vm((LEN + PROMPT, HD), BF),
        vm((HD, LEN + PROMPT), BF),
        vm((HD, LEN + PROMPT), BF),
        vm((LEN, HD), F32),
        vm((LEN, HD), F32),
        vm((LEN, FEAT), BF),
        vm((2, HALF, FEAT), BF),
        vm((LEN, 768), BF),
        vm((3, TOK, D), BF),
        vm((TOK, D), F32),
        vm((3, TOK, D), BF),
        vm((4, 8, COLS, FEAT), BF),
        vm((4, 8, COLS, FEAT), BF),
        vm((4, 8, COLS, FEAT), F32),
        vm((4, 8, COLS, FEAT), BF),
        vm((3, 8, COLS, FEAT), BF),
        vm((8, COLS, FEAT), BF),
        vm((7, COLS, FEAT), BF),
        pltpu.SemaphoreType.DMA((N_COPIES,)),
        pltpu.SemaphoreType.DMA((N_COPIES,)),
        pltpu.SemaphoreType.DMA((1,)),
    ]
    block_out, qkv_grad, w_grad_t = pl.pallas_call(
        body,
        out_shape=(
            jax.ShapeDtypeStruct((TOK, D), BF),
            jax.ShapeDtypeStruct((TOK, H * 3 * HD), BF),
            jax.ShapeDtypeStruct((COLS, FEAT), F32),
        ),
        in_specs=[vmem] * 8 + [anym],
        out_specs=(vmem, vmem, vmem),
        scratch_shapes=scratch,
        name="block",
        cost_estimate=pl.CostEstimate(flops=12_000_000_000, bytes_accessed=10_000_000, transcendentals=3_200_000),
        compiler_params=pltpu.CompilerParams(
            collective_id=0, has_side_effects=True, vmem_limit_bytes=60 * 1024 * 1024
        ),
    )(
        gate_row, t5_gain[None], out_cotangent[0], clip_input[0], prompt_states[0], prompt_ids,
        w_text, w_out.T, qkv_input[0],
    )
    return block_out[None], qkv_grad[None], w_grad_t.T


def solution(mesh):
    in_specs = (
        P(("grp", "fsdp"), "seq", None),
        P(("grp", "fsdp"), "seq", None),
        P(("grp", "fsdp"), "seq", None),
        P(("grp", "fsdp"), "seq"),
        P(),
        P("seq", ("grp", "fsdp")),
        P("seq", ("grp", "fsdp")),
        P(),
        P(("grp", "fsdp")),
        P(("grp", "fsdp"), "seq", None),
    )
    out_specs = (
        P(("grp", "fsdp"), "seq", None),
        P(("grp", "fsdp"), "seq", None),
        P("seq", ("grp", "fsdp")),
    )
    return jax.shard_map(
        per_device, mesh=mesh, in_specs=in_specs, out_specs=out_specs, check_vma=False
    )
```

```python
import functools
import math

import jax
import jax.numpy as jnp
from jax import lax
from jax.experimental import pallas as pl
from jax.experimental.pallas import tpu as pltpu
from jax.sharding import PartitionSpec as P

H = 16
HD = 128
D = 3072
DT = 4096
LEN = 1024
PROMPT = 512
TOK = 128
PTOK = 64
HALF = 512
PHALF = 256
FEAT = 256
COLS = 96
KC = 512

MESH = pl.DeviceIdType.MESH
BF = jnp.bfloat16
F32 = jnp.float32

norm_eps = 1e-06
masked_score = -1e30
score_scale = 1.0 / math.sqrt(HD)
log2e = math.log2(math.e)

N_COPIES = 140


def nt(a, b):
    return lax.dot_general(a, b, (((1,), (1,)), ((), ())), preferred_element_type=F32)


def nn(a, b):
    return lax.dot_general(a, b, (((1,), (0,)), ((), ())), preferred_element_type=F32)


def body(
    gate, gain, cot, clip, prm, ids, wtin, woin, qkv,
    bo, dqo, wgo,
    wt, wo, pg, pgt, nrm, cnts, qkvs, dos, dosend, tkv, tksend,
    kb, vb, kt, vt, probs, att, aabs, dqs,
    pp, pa, pf, pown, wsend, wrecv, wxs, wxr, wzs, wzr,
    send_sem, recv_sem, loc_sem,
):
    g = lax.axis_index("grp")
    f = lax.axis_index("fsdp")
    s = lax.axis_index("seq")
    zlo, x = lax.div(f, 4), lax.rem(f, 4)
    zhi, y = lax.div(s, 4), lax.rem(s, 4)
    z = zhi * 4 + zlo
    ozhi = 1 - zhi

    def at(gg, xx, yy, zz):
        return (gg, lax.rem(zz, 4) * 4 + xx, lax.div(zz, 4) * 4 + yy)

    sib = at(1 - g, x, y, z)
    xd = [at(g, lax.rem(x + j, 4), y, z) for j in range(4)]
    yd = [at(g, x, lax.rem(y + j, 4), z) for j in range(4)]
    zd = [at(g, x, y, lax.rem(z + j, 8)) for j in range(8)]
    clip_peers = []
    for dz in range(2):
        for dy in range(4):
            if dz or dy:
                py, pz = lax.rem(y + dy, 4), lax.rem(z + 4 * dz, 8)
                clip_peers.append((at(g, x, py, pz), lax.div(pz, 4) * 4 + py))
    partner = zd[4]
    peers = [sib] + xd[1:] + zd[1:] + [clip_peers[i][0] for i in (0, 1, 2, 4, 5, 6)]

    barrier = pltpu.get_barrier_semaphore()
    for p in peers:
        pl.semaphore_signal(barrier, inc=1, device_id=p, device_id_type=MESH)

    started = []

    def send(src, dst, device):
        i = len(started)
        c = pltpu.make_async_remote_copy(
            src_ref=src, dst_ref=dst, send_sem=send_sem.at[i], recv_sem=recv_sem.at[i],
            device_id=device, device_id_type=MESH,
        )
        c.start()
        started.append(c)
        return c

    def slot(zz):
        d = lax.rem(zz - z + 8, 8)
        return jnp.minimum(2 * d, 15 - 2 * d)

    wo[g, x, 0] = woin[...]
    wt[g, x, 0] = wtin[...]
    gate_row = gate[...].astype(F32)
    my_rows = pl.ds(pl.multiple_of(y * TOK, TOK), TOK)
    pg[my_rows, :] = (gate_row * cot[...].astype(F32)).astype(BF)
    my_prompt = pl.ds(pl.multiple_of(y * PTOK, PTOK), PTOK)
    wide = prm[...].astype(F32)
    mean = jnp.mean(wide * wide, axis=-1, keepdims=True)
    nrm[my_prompt, :] = (wide * lax.rsqrt(mean + norm_eps) * gain[...]).astype(BF)
    live = jnp.sum((ids[...] != 0).astype(jnp.int32), axis=-1, keepdims=True)
    cnts[0] = jnp.broadcast_to(live, (8, 128))

    pl.semaphore_wait(barrier, len(peers))

    def zstep(buf, k):
        if k < 4:
            a, b = (0, 0) if k == 1 else (2 * k - 3, 2 * k - 2)
            return [
                send(buf.at[g, x, a], buf.at[g, x, 2 * k - 1], zd[1]),
                send(buf.at[g, x, b], buf.at[g, x, 2 * k], zd[7]),
            ]
        h = buf.shape[3] // 2
        top, bottom = pl.ds(0, h), pl.ds(h, h)
        return [
            send(buf.at[g, x, 5, top], buf.at[g, x, 7, top], zd[1]),
            send(buf.at[g, x, 6, bottom], buf.at[g, x, 7, bottom], zd[7]),
        ]

    groups = ((0, 1), (1, 2), (3, 2), (5, 2), (7, 1))

    def xfirst(buf, k):
        sl = pl.ds(*groups[k])
        mine = buf.at[g, x, sl]
        return [send(mine, mine, xd[1]), send(mine, mine, xd[3])]

    def xsecond(buf, k):
        first, n = groups[k]
        lx, rx = lax.rem(x + 3, 4), lax.rem(x + 1, 4)
        if n == 2:
            from_left, from_right = buf.at[g, lx, first], buf.at[g, rx, first + 1]
        else:
            h = buf.shape[3] // 2
            from_left = buf.at[g, lx, first, pl.ds(0, h)]
            from_right = buf.at[g, rx, first, pl.ds(h, h)]
        return [send(from_left, from_left, xd[1]), send(from_right, from_right, xd[3])]

    def to_sibling(buf, k):
        both = buf.at[g, :, pl.ds(*groups[k])]
        return [send(both, both, sib)]

    def got(copies):
        for c in copies:
            c.wait_recv()

    def yfirst(buf, n):
        mine = buf.at[pl.ds(pl.multiple_of(y * n, n), n), :]
        return [send(mine, mine, yd[1]), send(mine, mine, yd[3])]

    def ysecond(buf, n):
        h = n // 2
        from_left = buf.at[pl.ds(pl.multiple_of(lax.rem(y + 3, 4) * n, n), h), :]
        from_right = buf.at[pl.ds(pl.multiple_of(lax.rem(y + 1, 4) * n + h, h), h), :]
        return [send(from_left, from_left, yd[1]), send(from_right, from_right, yd[3])]

    zt, zo, xt, xt2, st = {}, {}, {}, {}, {}
    zt[1] = zstep(wt, 1)
    xt[0] = xfirst(wt, 0)
    zo[1] = zstep(wo, 1)
    pg1 = yfirst(pg, TOK)
    n1 = yfirst(nrm, PTOK)
    cnt_copies = [
        send(cnts.at[0], cnts.at[i + 1], dev) for i, (dev, _) in enumerate(clip_peers)
    ]
    my_token_rows = pl.ds(pl.multiple_of(s * TOK, TOK), TOK)
    own_qkv = pltpu.make_async_copy(
        qkv.at[:, pl.ds(pl.multiple_of(s * 768, 768), 768)], qkvs.at[my_token_rows, :], loc_sem.at[0]
    )
    own_qkv.start()

    for k in range(1, 5):
        got(zt[k])
        if k < 4:
            zt[k + 1] = zstep(wt, k + 1)
        xt[k] = xfirst(wt, k)
        got(zo[k])
        if k < 4:
            zo[k + 1] = zstep(wo, k + 1)
        if k == 3:
            qkv_copies = []
            for dev, ps in reversed(clip_peers):
                cols = pl.ds(pl.multiple_of(ps * 768, 768), 768)
                qkv_copies.append(send(qkv.at[:, cols], qkvs.at[my_token_rows, :], dev))
            got(pg1)
            pg2 = ysecond(pg, TOK)
        if k == 4:
            mine = wo.at[g, x]
            xo = [send(mine, mine, xd[1]), send(mine, mine, xd[3])]
            got(n1)
            n2 = ysecond(nrm, PTOK)
        got(xt[k - 1])
        xt2[k - 1] = xsecond(wt, k - 1)
        if k >= 2:
            got(xt2[k - 2])
            st[k - 2] = to_sibling(wt, k - 2)
    got(xt[4])
    xt2[4] = xsecond(wt, 4)
    for k in (3, 4):
        got(xt2[k])
        st[k] = to_sibling(wt, k)
    got(n2)
    got(xo)
    from_left = wo.at[g, lax.rem(x + 3, 4), pl.ds(0, 4)]
    from_right = wo.at[g, lax.rem(x + 1, 4), pl.ds(4, 4)]
    xo2 = [send(from_left, from_left, xd[1]), send(from_right, from_right, xd[3])]
    for k in range(5):
        got(st[k])

    def prompt_kv(zh, dst, row0):
        def rows(i, carry):
            acc = jnp.zeros((128, 512), F32)
            here = pl.ds(pl.multiple_of(i * 128, 128), 128)
            for gg in range(2):
                for q in range(4):
                    sl = slot(zh * 4 + q)
                    w = jnp.concatenate([wt[gg, xx, sl] for xx in range(4)], axis=1)
                    acc += nt(nrm[here, pl.ds((gg * 4 + q) * 512, 512)], w)
            dst[pl.ds(pl.multiple_of(row0 + i * 128, 128), 128), :] = acc.astype(BF)
            return carry

        lax.fori_loop(0, PHALF // 128, rows, 0)

    prompt_kv(ozhi, tksend, 0)
    tk_copy = send(tksend, tkv.at[pl.ds(pl.multiple_of(zhi * PHALF, PHALF), PHALF), :], partner)
    prompt_kv(zhi, tkv, zhi * PHALF)
    got(xo2)
    both = wo.at[g]
    so = send(both, both, sib)
    got(pg2)

    def turn(i, carry):
        c = pl.ds(pl.multiple_of(i * 128, 128), 128)
        pgt[c, :] = pg[:, c].T
        return carry

    lax.fori_loop(0, D // 128, turn, 0)
    so.wait_recv()

    def attended_grad(zh, dst, row0):
        def rows(i, carry):
            acc = jnp.zeros((TOK, FEAT), F32)
            here = pl.ds(pl.multiple_of(i * TOK, TOK), TOK)
            for gg in range(2):
                for q in range(4):
                    w = wo[gg, :, slot(zh * 4 + q)].reshape(4 * COLS, FEAT)
                    acc += nn(pg[here, pl.ds((gg * 4 + q) * 384, 384)], w)
            dst[pl.ds(pl.multiple_of(row0 + i * TOK, TOK), TOK), :] = acc.astype(BF)
            return carry

        lax.fori_loop(0, HALF // TOK, rows, 0)

    attended_grad(ozhi, dosend, 0)
    half_rows = pl.ds(pl.multiple_of(zhi * HALF, HALF), HALF)
    do_copy = send(dosend, dos.at[half_rows, :], partner)
    attended_grad(zhi, dos, zhi * HALF)

    got(cnt_copies)
    total = cnts[0]
    for i in range(1, 8):
        total += cnts[i]
    live_row = total[0:1, 0:1]
    own_qkv.wait()
    got(qkv_copies)
    tk_copy.wait_recv()

    for h in range(2):
        kb[h, pl.ds(0, LEN), :] = qkvs[:, pl.ds(h * 384 + 128, 128)]
        vb[h, pl.ds(0, LEN), :] = qkvs[:, pl.ds(h * 384 + 256, 128)]
        kb[h, pl.ds(LEN, PROMPT), :] = tkv[:, pl.ds(h * 256, 128)]
        vb[h, pl.ds(LEN, PROMPT), :] = tkv[:, pl.ds(h * 256 + 128, 128)]
        kt[h] = kb[h].T
        vt[h] = vb[h].T

    chunks = [(c, c + KC) for c in range(0, LEN + PROMPT, KC)]

    def forward(half):
        here = pl.ds(pl.multiple_of(half * HALF, HALF), HALF)
        for h in range(2):
            q = qkvs[here, pl.ds(h * 384, 128)]
            scores, peak = [], None
            for lo, hi in chunks:
                t = nt(kb[h, lo:hi, :], q) * (score_scale * log2e)
                if lo >= LEN:
                    row = lax.broadcasted_iota(jnp.int32, t.shape, 0) + (lo - LEN)
                    t = jnp.where(row < live_row, t, masked_score)
                top = jnp.max(t, axis=0, keepdims=True)
                peak = top if peak is None else jnp.maximum(peak, top)
                scores.append(t)
            weights, norm = [], None
            for t in scores:
                e = jnp.exp2(t - peak)
                part = jnp.sum(e, axis=0, keepdims=True)
                norm = part if norm is None else norm + part
                weights.append(e)
            inv = 1.0 / norm
            o_t = None
            for (lo, hi), e in zip(chunks, weights):
                p = (e * inv).astype(BF)
                probs[h, lo:hi, here] = p
                term = nn(vt[h, :, lo:hi], p)
                o_t = term if o_t is None else o_t + term
            att[here, pl.ds(h * 128, 128)] = o_t.T.astype(BF)

    def backward(h):
        q = qkvs[:, pl.ds(h * 384, 128)]
        do = dos[:, pl.ds(h * 128, 128)]
        prod = do.astype(F32) * att[:, pl.ds(h * 128, 128)].astype(F32)
        row_dot = jnp.sum(prod.T, axis=0, keepdims=True)
        dq_t = None
        for lo, hi in chunks:
            p = probs[h, lo:hi, :]
            ds = (p.astype(F32) * (nt(vb[h, lo:hi, :], do) - row_dot)).astype(BF)
            term = nn(kt[h, :, lo:hi], ds)
            dq_t = term if dq_t is None else dq_t + term
            if hi <= LEN:
                dqs[lo:hi, pl.ds(h * 384 + 128, 128)] = (nn(ds, q) * score_scale).astype(BF)
                dqs[lo:hi, pl.ds(h * 384 + 256, 128)] = nn(p, do).astype(BF)
        dqs[:, pl.ds(h * 384, 128)] = (dq_t * score_scale).T.astype(BF)

    forward(ozhi)
    theirs = pl.ds(pl.multiple_of(ozhi * HALF, HALF), HALF)
    att_copy = send(att.at[theirs, :], aabs.at[zhi], partner)
    forward(zhi)
    aabs[zhi] = att[half_rows, :]
    do_copy.wait_recv()
    dq_copies = []
    for h in range(2):
        backward(h)
        hq = pl.ds(h * 384, 384)
        out_cols = pl.ds(pl.multiple_of(s * 768 + h * 384, 384), 384)
        for dev, ps in reversed(clip_peers):
            rows = pl.ds(pl.multiple_of(ps * TOK, TOK), TOK)
            dq_copies.append(send(dqs.at[rows, hq], dqo.at[:, out_cols], dev))
        dqo[:, out_cols] = dqs[my_token_rows, hq]

    att_copy.wait_recv()

    def project(rows, put):
        for gg in range(2):
            for q in range(4):
                acc = None
                for zh in range(2):
                    w = wo[gg, :, slot(zh * 4 + q)].reshape(4 * COLS, FEAT)
                    term = nt(aabs[zh, rows, :], w)
                    acc = term if acc is None else acc + term
                put(pl.ds((gg * 4 + q) * 384, 384), acc)

    def project_for(j):
        def put(c, v):
            pp[j - 1, :, c] = v.astype(BF)

        project(pl.ds(pl.multiple_of(lax.rem(y + j, 4) * TOK, TOK), TOK), put)

    first, second = pl.ds(0, TOK // 2), pl.ds(TOK // 2, TOK // 2)
    project_for(2)
    p_far = [
        send(pp.at[1, first], pa.at[0], yd[1]),
        send(pp.at[1, second], pa.at[1], yd[3]),
    ]
    project_for(1)
    p_near = [send(pp.at[0, second], pf.at[0, second], yd[1])]
    project_for(3)
    p_near.append(send(pp.at[2, first], pf.at[1, first], yd[3]))

    def weight_grad(gg, put):
        def group(q, carry):
            rows = pl.ds(pl.multiple_of((gg * 4 + q) * 384, 384), 384)
            for zh in range(2):
                put(zh * 4 + q, nn(pgt[rows, :], aabs[zh]).reshape(4, COLS, FEAT))
            return carry

        lax.fori_loop(0, 4, group, 0)

    def put_sibling(zz, v):
        wsend[:, zz] = v.astype(BF)

    weight_grad(1 - g, put_sibling)
    w_copy = send(wsend, wrecv, sib)

    p_far[0].wait_recv()
    pp[0, first] = (pp[0, first].astype(F32) + pa[0].astype(F32)).astype(BF)
    p_near.append(send(pp.at[0, first], pf.at[0, first], yd[1]))
    p_far[1].wait_recv()
    pp[2, second] = (pp[2, second].astype(F32) + pa[1].astype(F32)).astype(BF)
    p_near.append(send(pp.at[2, second], pf.at[1, second], yd[3]))

    w_copy.wait_recv()

    def put_chip(zz, v):
        wxs[:, zz] = (v + wrecv[:, zz].astype(F32)).astype(BF)

    weight_grad(g, put_chip)
    wx_copies = [send(wxs.at[lax.rem(x + j, 4)], wxr.at[j - 1], xd[j]) for j in (2, 1, 3)]

    def put_own(c, v):
        pown[:, c] = v

    project(my_rows, put_own)

    got(wx_copies)

    def x_sum(i, carry):
        v = wxs[x, i].astype(F32)
        for j in range(3):
            v += wxr[j, i].astype(F32)
        wzs[i] = v.astype(BF)
        return carry

    lax.fori_loop(0, 8, x_sum, 0)
    wz_copies = [send(wzs.at[lax.rem(z + j, 8)], wzr.at[j - 1], zd[j]) for j in (4, 3, 5, 2, 6, 1, 7)]

    got(p_near)
    proj = pown[...] + pf[0].astype(F32) + pf[1].astype(F32)
    bo[...] = (clip[...].astype(F32) + gate_row * proj).astype(BF)

    got(wz_copies)
    v = wzs[z].astype(F32)
    for j in range(7):
        v += wzr[j].astype(F32)
    wgo[...] = v

    got(dq_copies)
    for c in started:
        c.wait_send()


def per_device(
    clip_input, qkv_input, prompt_states, prompt_ids, t5_gain, w_text, w_out, gate_table,
    timesteps, out_cotangent,
):
    gate_row = lax.dynamic_index_in_dim(gate_table, timesteps[0], 0, keepdims=True)
    vmem = pl.BlockSpec(memory_space=pltpu.VMEM)
    anym = pl.BlockSpec(memory_space=pl.ANY)
    vm = pltpu.VMEM
    scratch = [
        vm((2, 4, 8, 512, 128), BF),
        vm((2, 4, 8, COLS, FEAT), BF),
        vm((HALF, D), BF),
        vm((D, HALF), BF),
        vm((PHALF, DT), BF),
        vm((8, 8, 128), jnp.int32),
        vm((LEN, 768), BF),
        vm((LEN, FEAT), BF),
        vm((HALF, FEAT), BF),
        vm((PROMPT, 512), BF),
        vm((PHALF, 512), BF),
        vm((2, LEN + PROMPT, HD), BF),
        vm((2, LEN + PROMPT, HD), BF),
        vm((2, HD, LEN + PROMPT), BF),
        vm((2, HD, LEN + PROMPT), BF),
        vm((2, LEN + PROMPT, LEN), BF),
        vm((LEN, FEAT), BF),
        vm((2, HALF, FEAT), BF),
        vm((LEN, 768), BF),
        vm((3, TOK, D), BF),
        vm((2, TOK // 2, D), BF),
        vm((2, TOK, D), BF),
        vm((TOK, D), F32),
        vm((4, 8, COLS, FEAT), BF),
        vm((4, 8, COLS, FEAT), BF),
        vm((4, 8, COLS, FEAT), BF),
        vm((3, 8, COLS, FEAT), BF),
        vm((8, COLS, FEAT), BF),
        vm((7, COLS, FEAT), BF),
        pltpu.SemaphoreType.DMA((N_COPIES,)),
        pltpu.SemaphoreType.DMA((N_COPIES,)),
        pltpu.SemaphoreType.DMA((1,)),
    ]
    block_out, qkv_grad, w_grad_t = pl.pallas_call(
        body,
        out_shape=(
            jax.ShapeDtypeStruct((TOK, D), BF),
            jax.ShapeDtypeStruct((TOK, H * 3 * HD), BF),
            jax.ShapeDtypeStruct((COLS, FEAT), F32),
        ),
        in_specs=[vmem] * 8 + [anym],
        out_specs=(vmem, vmem, vmem),
        scratch_shapes=scratch,
        name="block",
        cost_estimate=pl.CostEstimate(flops=12_000_000_000, bytes_accessed=10_000_000, transcendentals=3_200_000),
        compiler_params=pltpu.CompilerParams(
            collective_id=0, has_side_effects=True, vmem_limit_bytes=60 * 1024 * 1024
        ),
    )(
        gate_row, t5_gain[None], out_cotangent[0], clip_input[0], prompt_states[0], prompt_ids,
        w_text, w_out.T, qkv_input[0],
    )
    return block_out[None], qkv_grad[None], w_grad_t.T


def solution(mesh):
    in_specs = (
        P(("grp", "fsdp"), "seq", None),
        P(("grp", "fsdp"), "seq", None),
        P(("grp", "fsdp"), "seq", None),
        P(("grp", "fsdp"), "seq"),
        P(),
        P("seq", ("grp", "fsdp")),
        P("seq", ("grp", "fsdp")),
        P(),
        P(("grp", "fsdp")),
        P(("grp", "fsdp"), "seq", None),
    )
    out_specs = (
        P(("grp", "fsdp"), "seq", None),
        P(("grp", "fsdp"), "seq", None),
        P("seq", ("grp", "fsdp")),
    )
    return jax.shard_map(
        per_device, mesh=mesh, in_specs=in_specs, out_specs=out_specs, check_vma=False
    )
```

```python
import functools
import math

import jax
import jax.numpy as jnp
from jax import lax
from jax.experimental import pallas as pl
from jax.experimental.pallas import tpu as pltpu
from jax.sharding import PartitionSpec as P

H = 16
HD = 128
D = 3072
DT = 4096
LEN = 1024
PROMPT = 512
TOK = 128
PTOK = 64
HALF = 512
PHALF = 256
FEAT = 256
COLS = 96
KC = 512

MESH = pl.DeviceIdType.MESH
BF = jnp.bfloat16
F32 = jnp.float32

norm_eps = 1e-06
masked_score = -1e30
score_scale = 1.0 / math.sqrt(HD)
log2e = math.log2(math.e)

N_COPIES = 140


def nt(a, b):
    return lax.dot_general(a, b, (((1,), (1,)), ((), ())), preferred_element_type=F32)


def nn(a, b):
    return lax.dot_general(a, b, (((1,), (0,)), ((), ())), preferred_element_type=F32)


def body(
    gate, gain, cot, clip, prm, ids, wtin, woin, qkv,
    bo, dqo, wgo,
    wt, wo, pg, pgt, nrm, cnts, qkvs, dos, dosend, tkv, tksend,
    kb, vb, kt, vt, probs, att, aabs, dqs,
    pp, pa, pf, pown, wsend, wrecv, wxs, wxr, wzs, wzr,
    send_sem, recv_sem, loc_sem,
):
    g = lax.axis_index("grp")
    f = lax.axis_index("fsdp")
    s = lax.axis_index("seq")
    zlo, x = lax.div(f, 4), lax.rem(f, 4)
    zhi, y = lax.div(s, 4), lax.rem(s, 4)
    z = zhi * 4 + zlo
    ozhi = 1 - zhi

    def at(gg, xx, yy, zz):
        return (gg, lax.rem(zz, 4) * 4 + xx, lax.div(zz, 4) * 4 + yy)

    sib = at(1 - g, x, y, z)
    xd = [at(g, lax.rem(x + j, 4), y, z) for j in range(4)]
    yd = [at(g, x, lax.rem(y + j, 4), z) for j in range(4)]
    zd = [at(g, x, y, lax.rem(z + j, 8)) for j in range(8)]
    clip_peers = []
    for dz in range(2):
        for dy in range(4):
            if dz or dy:
                py, pz = lax.rem(y + dy, 4), lax.rem(z + 4 * dz, 8)
                clip_peers.append((at(g, x, py, pz), lax.div(pz, 4) * 4 + py))
    partner = zd[4]
    peers = [sib] + xd[1:] + zd[1:] + [clip_peers[i][0] for i in (0, 1, 2, 4, 5, 6)]

    barrier = pltpu.get_barrier_semaphore()
    for p in peers:
        pl.semaphore_signal(barrier, inc=1, device_id=p, device_id_type=MESH)

    started = []

    def send(src, dst, device):
        i = len(started)
        c = pltpu.make_async_remote_copy(
            src_ref=src, dst_ref=dst, send_sem=send_sem.at[i], recv_sem=recv_sem.at[i],
            device_id=device, device_id_type=MESH,
        )
        c.start()
        started.append(c)
        return c

    def slot(zz):
        d = lax.rem(zz - z + 8, 8)
        return jnp.minimum(2 * d, 15 - 2 * d)

    wo[g, x, 0] = woin[...]
    wt[g, x, 0] = wtin[...]
    pl.semaphore_wait(barrier, len(peers))

    def zstep(buf, k):
        if k < 4:
            a, b = (0, 0) if k == 1 else (2 * k - 3, 2 * k - 2)
            return [
                send(buf.at[g, x, a], buf.at[g, x, 2 * k - 1], zd[1]),
                send(buf.at[g, x, b], buf.at[g, x, 2 * k], zd[7]),
            ]
        h = buf.shape[3] // 2
        top, bottom = pl.ds(0, h), pl.ds(h, h)
        return [
            send(buf.at[g, x, 5, top], buf.at[g, x, 7, top], zd[1]),
            send(buf.at[g, x, 6, bottom], buf.at[g, x, 7, bottom], zd[7]),
        ]

    groups = ((0, 1), (1, 2), (3, 2), (5, 2), (7, 1))

    def xfirst(buf, k):
        sl = pl.ds(*groups[k])
        mine = buf.at[g, x, sl]
        return [send(mine, mine, xd[1]), send(mine, mine, xd[3])]

    def xsecond(buf, k):
        first, n = groups[k]
        lx, rx = lax.rem(x + 3, 4), lax.rem(x + 1, 4)
        if n == 2:
            from_left, from_right = buf.at[g, lx, first], buf.at[g, rx, first + 1]
        else:
            h = buf.shape[3] // 2
            from_left = buf.at[g, lx, first, pl.ds(0, h)]
            from_right = buf.at[g, rx, first, pl.ds(h, h)]
        return [send(from_left, from_left, xd[1]), send(from_right, from_right, xd[3])]

    def to_sibling(buf, k):
        both = buf.at[g, :, pl.ds(*groups[k])]
        return [send(both, both, sib)]

    def got(copies):
        for c in copies:
            c.wait_recv()

    def yfirst(buf, n):
        mine = buf.at[pl.ds(pl.multiple_of(y * n, n), n), :]
        return [send(mine, mine, yd[1]), send(mine, mine, yd[3])]

    def ysecond(buf, n):
        h = n // 2
        from_left = buf.at[pl.ds(pl.multiple_of(lax.rem(y + 3, 4) * n, n), h), :]
        from_right = buf.at[pl.ds(pl.multiple_of(lax.rem(y + 1, 4) * n + h, h), h), :]
        return [send(from_left, from_left, yd[1]), send(from_right, from_right, yd[3])]

    zt, zo, xt, xt2, st = {}, {}, {}, {}, {}
    qkv_copies = []

    def send_qkv(peer, part=0, parts=1):
        dev, ps = clip_peers[peer]
        n = TOK // parts
        qkv_copies.append(
            send(
                qkv.at[pl.ds(part * n, n), pl.ds(pl.multiple_of(ps * 768, 768), 768)],
                qkvs.at[pl.ds(pl.multiple_of(s * TOK + part * n, n), n), :],
                dev,
            )
        )

    zt[1] = zstep(wt, 1)
    xt[0] = xfirst(wt, 0)
    zo[1] = zstep(wo, 1)
    send_qkv(3, 0, 4)
    my_prompt = pl.ds(pl.multiple_of(y * PTOK, PTOK), PTOK)
    wide = prm[...].astype(F32)
    mean = jnp.mean(wide * wide, axis=-1, keepdims=True)
    nrm[my_prompt, :] = (wide * lax.rsqrt(mean + norm_eps) * gain[...]).astype(BF)
    n1 = yfirst(nrm, PTOK)
    gate_row = gate[...].astype(F32)
    my_rows = pl.ds(pl.multiple_of(y * TOK, TOK), TOK)
    pg[my_rows, :] = (gate_row * cot[...].astype(F32)).astype(BF)
    live = jnp.sum((ids[...] != 0).astype(jnp.int32), axis=-1, keepdims=True)
    cnts[0] = jnp.broadcast_to(live, (8, 128))
    cnt_copies = [
        send(cnts.at[0], cnts.at[i + 1], dev) for i, (dev, _) in enumerate(clip_peers)
    ]
    my_token_rows = pl.ds(pl.multiple_of(s * TOK, TOK), TOK)
    own_qkv = pltpu.make_async_copy(
        qkv.at[:, pl.ds(pl.multiple_of(s * 768, 768), 768)], qkvs.at[my_token_rows, :], loc_sem.at[0]
    )
    own_qkv.start()

    for k in range(1, 5):
        got(zt[k])
        if k < 4:
            zt[k + 1] = zstep(wt, k + 1)
        xt[k] = xfirst(wt, k)
        got(zo[k])
        if k < 4:
            zo[k + 1] = zstep(wo, k + 1)
            send_qkv(3, k, 4)
        else:
            for peer in (6, 5, 4):
                send_qkv(peer)
        if k == 2:
            got(n1)
            n2 = ysecond(nrm, PTOK)
            pg1 = yfirst(pg, TOK)
        got(xt[k - 1])
        xt2[k - 1] = xsecond(wt, k - 1)
        if k >= 2:
            got(xt2[k - 2])
            st[k - 2] = to_sibling(wt, k - 2)
    got(pg1)
    pg2 = ysecond(pg, TOK)
    for peer in (2, 1, 0):
        send_qkv(peer)
    got(xt[4])
    xt2[4] = xsecond(wt, 4)
    mine = wo.at[g, x]
    xo = [send(mine, mine, xd[1]), send(mine, mine, xd[3])]
    got(xt2[3])
    st[3] = to_sibling(wt, 3)
    got(xt2[4])
    st[4] = to_sibling(wt, 4)
    got(n2)
    for k in range(5):
        got(st[k])

    def prompt_kv(zh, dst, row0):
        acc = jnp.zeros((PHALF, 512), F32)
        for gg in range(2):
            for q in range(4):
                sl = slot(zh * 4 + q)
                w = jnp.concatenate([wt[gg, xx, sl] for xx in range(4)], axis=1)
                acc += nt(nrm[:, pl.ds((gg * 4 + q) * 512, 512)], w)
        dst[pl.ds(pl.multiple_of(row0, PHALF), PHALF), :] = acc.astype(BF)

    prompt_kv(ozhi, tksend, 0)
    tk_copy = send(tksend, tkv.at[pl.ds(pl.multiple_of(zhi * PHALF, PHALF), PHALF), :], partner)
    got(xo)
    from_left = wo.at[g, lax.rem(x + 3, 4), pl.ds(0, 4)]
    from_right = wo.at[g, lax.rem(x + 1, 4), pl.ds(4, 4)]
    xo2 = [send(from_left, from_left, xd[1]), send(from_right, from_right, xd[3])]
    prompt_kv(zhi, tkv, zhi * PHALF)
    got(xo2)
    both = wo.at[g]
    so = send(both, both, sib)
    got(pg2)

    so.wait_recv()

    def attended_grad(zh, dst, row0):
        acc = jnp.zeros((HALF, FEAT), F32)
        for gg in range(2):
            for q in range(4):
                w = wo[gg, :, slot(zh * 4 + q)].reshape(4 * COLS, FEAT)
                acc += nn(pg[:, pl.ds((gg * 4 + q) * 384, 384)], w)
        dst[pl.ds(pl.multiple_of(row0, HALF), HALF), :] = acc.astype(BF)

    attended_grad(ozhi, dosend, 0)
    half_rows = pl.ds(pl.multiple_of(zhi * HALF, HALF), HALF)
    do_copy = send(dosend, dos.at[half_rows, :], partner)
    attended_grad(zhi, dos, zhi * HALF)

    def turn(i, carry):
        c = pl.ds(pl.multiple_of(i * 128, 128), 128)
        pgt[c, :] = pg[:, c].T
        return carry

    lax.fori_loop(0, D // 128, turn, 0)

    got(cnt_copies)
    total = cnts[0]
    for i in range(1, 8):
        total += cnts[i]
    live_row = total[0:1, 0:1]
    own_qkv.wait()
    got(qkv_copies)
    tk_copy.wait_recv()

    for h in range(2):
        kb[h, pl.ds(0, LEN), :] = qkvs[:, pl.ds(h * 384 + 128, 128)]
        vb[h, pl.ds(0, LEN), :] = qkvs[:, pl.ds(h * 384 + 256, 128)]
        kb[h, pl.ds(LEN, PROMPT), :] = tkv[:, pl.ds(h * 256, 128)]
        vb[h, pl.ds(LEN, PROMPT), :] = tkv[:, pl.ds(h * 256 + 128, 128)]
        kt[h] = kb[h].T
        vt[h] = vb[h].T

    chunks = [(c, c + KC) for c in range(0, LEN + PROMPT, KC)]

    def forward(half):
        here = pl.ds(pl.multiple_of(half * HALF, HALF), HALF)
        for h in range(2):
            q = qkvs[here, pl.ds(h * 384, 128)]
            scores, peak = [], None
            for lo, hi in chunks:
                t = nt(kb[h, lo:hi, :], q) * (score_scale * log2e)
                if lo >= LEN:
                    row = lax.broadcasted_iota(jnp.int32, t.shape, 0) + (lo - LEN)
                    t = jnp.where(row < live_row, t, masked_score)
                top = jnp.max(t, axis=0, keepdims=True)
                peak = top if peak is None else jnp.maximum(peak, top)
                scores.append(t)
            weights, norm = [], None
            for t in scores:
                e = jnp.exp2(t - peak)
                part = jnp.sum(e, axis=0, keepdims=True)
                norm = part if norm is None else norm + part
                weights.append(e)
            inv = 1.0 / norm
            o_t = None
            for (lo, hi), e in zip(chunks, weights):
                p = (e * inv).astype(BF)
                probs[h, lo:hi, here] = p
                term = nn(vt[h, :, lo:hi], p)
                o_t = term if o_t is None else o_t + term
            att[here, pl.ds(h * 128, 128)] = o_t.T.astype(BF)

    def backward(h):
        q = qkvs[:, pl.ds(h * 384, 128)]
        do = dos[:, pl.ds(h * 128, 128)]
        prod = do.astype(F32) * att[:, pl.ds(h * 128, 128)].astype(F32)
        row_dot = jnp.sum(prod.T, axis=0, keepdims=True)
        dq_t = None
        for lo, hi in chunks:
            p = probs[h, lo:hi, :]
            ds = (p.astype(F32) * (nt(vb[h, lo:hi, :], do) - row_dot)).astype(BF)
            term = nn(kt[h, :, lo:hi], ds)
            dq_t = term if dq_t is None else dq_t + term
            if hi <= LEN:
                dqs[lo:hi, pl.ds(h * 384 + 128, 128)] = (nn(ds, q) * score_scale).astype(BF)
                dqs[lo:hi, pl.ds(h * 384 + 256, 128)] = nn(p, do).astype(BF)
        dqs[:, pl.ds(h * 384, 128)] = (dq_t * score_scale).T.astype(BF)

    forward(ozhi)
    theirs = pl.ds(pl.multiple_of(ozhi * HALF, HALF), HALF)
    att_copy = send(att.at[theirs, :], aabs.at[zhi], partner)
    forward(zhi)
    aabs[zhi] = att[half_rows, :]
    do_copy.wait_recv()
    dq_copies = []

    def send_grad(h, dev, ps):
        rows = pl.ds(pl.multiple_of(ps * TOK, TOK), TOK)
        cols = pl.ds(pl.multiple_of(s * 768 + h * 384, 384), 384)
        dq_copies.append(send(dqs.at[rows, pl.ds(h * 384, 384)], dqo.at[:, cols], dev))

    for h in range(2):
        backward(h)
        for dev, ps in clip_peers[:3]:
            send_grad(h, dev, ps)
        dqo[:, pl.ds(pl.multiple_of(s * 768 + h * 384, 384), 384)] = dqs[
            my_token_rows, pl.ds(h * 384, 384)
        ]

    att_copy.wait_recv()
    for h in range(2):
        for dev, ps in reversed(clip_peers[3:]):
            send_grad(h, dev, ps)

    def project(rows, put):
        for gg in range(2):
            for q in range(4):
                acc = None
                for zh in range(2):
                    w = wo[gg, :, slot(zh * 4 + q)].reshape(4 * COLS, FEAT)
                    term = nt(aabs[zh, rows, :], w)
                    acc = term if acc is None else acc + term
                put(pl.ds((gg * 4 + q) * 384, 384), acc)

    def project_for(j):
        def put(c, v):
            pp[j - 1, :, c] = v.astype(BF)

        project(pl.ds(pl.multiple_of(lax.rem(y + j, 4) * TOK, TOK), TOK), put)

    first, second = pl.ds(0, TOK // 2), pl.ds(TOK // 2, TOK // 2)
    def weight_grad(gg, put):
        def group(q, carry):
            rows = pl.ds(pl.multiple_of((gg * 4 + q) * 384, 384), 384)
            for zh in range(2):
                put(zh * 4 + q, nn(pgt[rows, :], aabs[zh]).reshape(4, COLS, FEAT))
            return carry

        lax.fori_loop(0, 4, group, 0)

    def put_sibling(zz, v):
        wsend[:, zz] = v.astype(BF)

    weight_grad(1 - g, put_sibling)
    w_copy = send(wsend, wrecv, sib)
    project_for(2)
    p_far = [
        send(pp.at[1, first], pa.at[0], yd[1]),
        send(pp.at[1, second], pa.at[1], yd[3]),
    ]
    project_for(1)
    p_near = [send(pp.at[0, second], pf.at[0, second], yd[1])]
    project_for(3)
    p_near.append(send(pp.at[2, first], pf.at[1, first], yd[3]))

    w_copy.wait_recv()

    def put_chip(zz, v):
        wxs[:, zz] = (v + wrecv[:, zz].astype(F32)).astype(BF)

    weight_grad(g, put_chip)
    wx_copies = [send(wxs.at[lax.rem(x + j, 4)], wxr.at[j - 1], xd[j]) for j in (2, 1, 3)]

    p_far[0].wait_recv()
    pp[0, first] = (pp[0, first].astype(F32) + pa[0].astype(F32)).astype(BF)
    p_near.append(send(pp.at[0, first], pf.at[0, first], yd[1]))
    p_far[1].wait_recv()
    pp[2, second] = (pp[2, second].astype(F32) + pa[1].astype(F32)).astype(BF)
    p_near.append(send(pp.at[2, second], pf.at[1, second], yd[3]))

    def put_own(c, v):
        pown[:, c] = v

    project(my_rows, put_own)

    got(wx_copies)

    def x_sum(i, carry):
        v = wxs[x, i].astype(F32)
        for j in range(3):
            v += wxr[j, i].astype(F32)
        wzs[i] = v.astype(BF)
        return carry

    lax.fori_loop(0, 8, x_sum, 0)
    wz_copies = [send(wzs.at[lax.rem(z + j, 8)], wzr.at[j - 1], zd[j]) for j in (4, 3, 5, 2, 6, 1, 7)]

    got(p_near)
    proj = pown[...] + pf[0].astype(F32) + pf[1].astype(F32)
    bo[...] = (clip[...].astype(F32) + gate_row * proj).astype(BF)

    got(wz_copies)
    v = wzs[z].astype(F32)
    for j in range(7):
        v += wzr[j].astype(F32)
    wgo[...] = v

    got(dq_copies)
    for c in started:
        c.wait_send()


def per_device(
    clip_input, qkv_input, prompt_states, prompt_ids, t5_gain, w_text, w_out, gate_table,
    timesteps, out_cotangent,
):
    gate_row = lax.dynamic_index_in_dim(gate_table, timesteps[0], 0, keepdims=True)
    vmem = pl.BlockSpec(memory_space=pltpu.VMEM)
    anym = pl.BlockSpec(memory_space=pl.ANY)
    vm = pltpu.VMEM
    scratch = [
        vm((2, 4, 8, 512, 128), BF),
        vm((2, 4, 8, COLS, FEAT), BF),
        vm((HALF, D), BF),
        vm((D, HALF), BF),
        vm((PHALF, DT), BF),
        vm((8, 8, 128), jnp.int32),
        vm((LEN, 768), BF),
        vm((LEN, FEAT), BF),
        vm((HALF, FEAT), BF),
        vm((PROMPT, 512), BF),
        vm((PHALF, 512), BF),
        vm((2, LEN + PROMPT, HD), BF),
        vm((2, LEN + PROMPT, HD), BF),
        vm((2, HD, LEN + PROMPT), BF),
        vm((2, HD, LEN + PROMPT), BF),
        vm((2, LEN + PROMPT, LEN), BF),
        vm((LEN, FEAT), BF),
        vm((2, HALF, FEAT), BF),
        vm((LEN, 768), BF),
        vm((3, TOK, D), BF),
        vm((2, TOK // 2, D), BF),
        vm((2, TOK, D), BF),
        vm((TOK, D), F32),
        vm((4, 8, COLS, FEAT), BF),
        vm((4, 8, COLS, FEAT), BF),
        vm((4, 8, COLS, FEAT), BF),
        vm((3, 8, COLS, FEAT), BF),
        vm((8, COLS, FEAT), BF),
        vm((7, COLS, FEAT), BF),
        pltpu.SemaphoreType.DMA((N_COPIES,)),
        pltpu.SemaphoreType.DMA((N_COPIES,)),
        pltpu.SemaphoreType.DMA((1,)),
    ]
    block_out, qkv_grad, w_grad_t = pl.pallas_call(
        body,
        out_shape=(
            jax.ShapeDtypeStruct((TOK, D), BF),
            jax.ShapeDtypeStruct((TOK, H * 3 * HD), BF),
            jax.ShapeDtypeStruct((COLS, FEAT), F32),
        ),
        in_specs=[vmem] * 8 + [anym],
        out_specs=(vmem, vmem, vmem),
        scratch_shapes=scratch,
        name="block",
        cost_estimate=pl.CostEstimate(flops=12_000_000_000, bytes_accessed=10_000_000, transcendentals=3_200_000),
        compiler_params=pltpu.CompilerParams(
            collective_id=0, has_side_effects=True, vmem_limit_bytes=60 * 1024 * 1024
        ),
    )(
        gate_row, t5_gain[None], out_cotangent[0], clip_input[0], prompt_states[0], prompt_ids,
        w_text, w_out.T, qkv_input[0],
    )
    return block_out[None], qkv_grad[None], w_grad_t.T


def solution(mesh):
    in_specs = (
        P(("grp", "fsdp"), "seq", None),
        P(("grp", "fsdp"), "seq", None),
        P(("grp", "fsdp"), "seq", None),
        P(("grp", "fsdp"), "seq"),
        P(),
        P("seq", ("grp", "fsdp")),
        P("seq", ("grp", "fsdp")),
        P(),
        P(("grp", "fsdp")),
        P(("grp", "fsdp"), "seq", None),
    )
    out_specs = (
        P(("grp", "fsdp"), "seq", None),
        P(("grp", "fsdp"), "seq", None),
        P("seq", ("grp", "fsdp")),
    )
    return jax.shard_map(
        per_device, mesh=mesh, in_specs=in_specs, out_specs=out_specs, check_vma=False
    )
```

```python
import functools
import math

import jax
import jax.numpy as jnp
from jax import lax
from jax.experimental import pallas as pl
from jax.experimental.pallas import tpu as pltpu
from jax.sharding import PartitionSpec as P

H = 16
HD = 128
D = 3072
DT = 4096
LEN = 1024
PROMPT = 512
TOK = 128
PTOK = 64
HALF = 512
PHALF = 256
FEAT = 256
COLS = 96
KC = 512

MESH = pl.DeviceIdType.MESH
BF = jnp.bfloat16
F32 = jnp.float32

norm_eps = 1e-06
masked_score = -1e30
score_scale = 1.0 / math.sqrt(HD)
log2e = math.log2(math.e)

N_COPIES = 140


def nt(a, b):
    return lax.dot_general(a, b, (((1,), (1,)), ((), ())), preferred_element_type=F32)


def nn(a, b):
    return lax.dot_general(a, b, (((1,), (0,)), ((), ())), preferred_element_type=F32)


def body(
    gate, gain, cot, clip, prm, ids, wtin, woin, qkv,
    bo, dqo, wgo,
    wt, wo, pg, pgt, nrm, cnts, qkvs, dos, dosend, tkv, tksend,
    kb, vb, kt, vt, probs, att, aabs, dqs,
    pp, pa, pf, pown, wsend, wrecv, wxs, wxr, wzs, wz0, wzr,
    send_sem, recv_sem, loc_sem,
):
    g = lax.axis_index("grp")
    f = lax.axis_index("fsdp")
    s = lax.axis_index("seq")
    zlo, x = lax.div(f, 4), lax.rem(f, 4)
    zhi, y = lax.div(s, 4), lax.rem(s, 4)
    z = zhi * 4 + zlo
    ozhi = 1 - zhi

    def at(gg, xx, yy, zz):
        return (gg, lax.rem(zz, 4) * 4 + xx, lax.div(zz, 4) * 4 + yy)

    sib = at(1 - g, x, y, z)
    xd = [at(g, lax.rem(x + j, 4), y, z) for j in range(4)]
    yd = [at(g, x, lax.rem(y + j, 4), z) for j in range(4)]
    zd = [at(g, x, y, lax.rem(z + j, 8)) for j in range(8)]
    clip_peers = []
    for dz in range(2):
        for dy in range(4):
            if dz or dy:
                py, pz = lax.rem(y + dy, 4), lax.rem(z + 4 * dz, 8)
                clip_peers.append((at(g, x, py, pz), lax.div(pz, 4) * 4 + py))
    partner = zd[4]
    peers = [sib] + xd[1:] + zd[1:] + [clip_peers[i][0] for i in (0, 1, 2, 4, 5, 6)]

    barrier = pltpu.get_barrier_semaphore()
    for p in peers:
        pl.semaphore_signal(barrier, inc=1, device_id=p, device_id_type=MESH)

    started = []

    def send(src, dst, device):
        i = len(started)
        c = pltpu.make_async_remote_copy(
            src_ref=src, dst_ref=dst, send_sem=send_sem.at[i], recv_sem=recv_sem.at[i],
            device_id=device, device_id_type=MESH,
        )
        c.start()
        started.append(c)
        return c

    def slot(zz):
        d = lax.rem(zz - z + 8, 8)
        return jnp.minimum(2 * d, 15 - 2 * d)

    wo[g, x, 0] = woin[...]
    wt[g, x, 0] = wtin[...]
    pl.semaphore_wait(barrier, len(peers))

    def zstep(buf, k):
        if k < 4:
            a, b = (0, 0) if k == 1 else (2 * k - 3, 2 * k - 2)
            return [
                send(buf.at[g, x, a], buf.at[g, x, 2 * k - 1], zd[1]),
                send(buf.at[g, x, b], buf.at[g, x, 2 * k], zd[7]),
            ]
        h = buf.shape[3] // 2
        top, bottom = pl.ds(0, h), pl.ds(h, h)
        return [
            send(buf.at[g, x, 5, top], buf.at[g, x, 7, top], zd[1]),
            send(buf.at[g, x, 6, bottom], buf.at[g, x, 7, bottom], zd[7]),
        ]

    groups = ((0, 1), (1, 2), (3, 2), (5, 2), (7, 1))

    def xfirst(buf, k):
        sl = pl.ds(*groups[k])
        mine = buf.at[g, x, sl]
        return [send(mine, mine, xd[1]), send(mine, mine, xd[3])]

    def xsecond(buf, k):
        first, n = groups[k]
        lx, rx = lax.rem(x + 3, 4), lax.rem(x + 1, 4)
        if n == 2:
            from_left, from_right = buf.at[g, lx, first], buf.at[g, rx, first + 1]
        else:
            h = buf.shape[3] // 2
            from_left = buf.at[g, lx, first, pl.ds(0, h)]
            from_right = buf.at[g, rx, first, pl.ds(h, h)]
        return [send(from_left, from_left, xd[1]), send(from_right, from_right, xd[3])]

    def to_sibling(buf, k):
        both = buf.at[g, :, pl.ds(*groups[k])]
        return [send(both, both, sib)]

    def got(copies):
        for c in copies:
            c.wait_recv()

    def yfirst(buf, n):
        mine = buf.at[pl.ds(pl.multiple_of(y * n, n), n), :]
        return [send(mine, mine, yd[1]), send(mine, mine, yd[3])]

    def ysecond(buf, n):
        h = n // 2
        from_left = buf.at[pl.ds(pl.multiple_of(lax.rem(y + 3, 4) * n, n), h), :]
        from_right = buf.at[pl.ds(pl.multiple_of(lax.rem(y + 1, 4) * n + h, h), h), :]
        return [send(from_left, from_left, yd[1]), send(from_right, from_right, yd[3])]

    zt, zo, xt, xt2, st = {}, {}, {}, {}, {}
    qkv_copies = []

    def send_qkv(peer, part=0, parts=1):
        dev, ps = clip_peers[peer]
        n = TOK // parts
        qkv_copies.append(
            send(
                qkv.at[pl.ds(part * n, n), pl.ds(pl.multiple_of(ps * 768, 768), 768)],
                qkvs.at[pl.ds(pl.multiple_of(s * TOK + part * n, n), n), :],
                dev,
            )
        )

    zt[1] = zstep(wt, 1)
    xt[0] = xfirst(wt, 0)
    zo[1] = zstep(wo, 1)
    send_qkv(3, 0, 4)
    my_prompt = pl.ds(pl.multiple_of(y * PTOK, PTOK), PTOK)
    wide = prm[...].astype(F32)
    mean = jnp.mean(wide * wide, axis=-1, keepdims=True)
    nrm[my_prompt, :] = (wide * lax.rsqrt(mean + norm_eps) * gain[...]).astype(BF)
    n1 = yfirst(nrm, PTOK)
    gate_row = gate[...].astype(F32)
    my_rows = pl.ds(pl.multiple_of(y * TOK, TOK), TOK)
    pg[my_rows, :] = (gate_row * cot[...].astype(F32)).astype(BF)
    live = jnp.sum((ids[...] != 0).astype(jnp.int32), axis=-1, keepdims=True)
    cnts[0] = jnp.broadcast_to(live, (8, 128))
    cnt_copies = [
        send(cnts.at[0], cnts.at[i + 1], dev) for i, (dev, _) in enumerate(clip_peers)
    ]
    my_token_rows = pl.ds(pl.multiple_of(s * TOK, TOK), TOK)
    own_qkv = pltpu.make_async_copy(
        qkv.at[:, pl.ds(pl.multiple_of(s * 768, 768), 768)], qkvs.at[my_token_rows, :], loc_sem.at[0]
    )
    own_qkv.start()

    for k in range(1, 5):
        got(zt[k])
        if k < 4:
            zt[k + 1] = zstep(wt, k + 1)
        xt[k] = xfirst(wt, k)
        got(zo[k])
        if k < 4:
            zo[k + 1] = zstep(wo, k + 1)
            send_qkv(3, k, 4)
        else:
            for peer in (6, 5, 4):
                send_qkv(peer)
        if k == 2:
            got(n1)
            n2 = ysecond(nrm, PTOK)
            pg1 = yfirst(pg, TOK)
        got(xt[k - 1])
        xt2[k - 1] = xsecond(wt, k - 1)
        if k >= 2:
            got(xt2[k - 2])
            st[k - 2] = to_sibling(wt, k - 2)
    got(pg1)
    pg2 = ysecond(pg, TOK)
    for peer in (2, 1, 0):
        send_qkv(peer)
    got(xt[4])
    xt2[4] = xsecond(wt, 4)
    mine = wo.at[g, x]
    xo = [send(mine, mine, xd[1]), send(mine, mine, xd[3])]
    got(xt2[3])
    st[3] = to_sibling(wt, 3)
    got(xt2[4])
    st[4] = to_sibling(wt, 4)
    got(n2)
    for k in range(5):
        got(st[k])

    def prompt_kv(zh, dst, row0):
        acc = jnp.zeros((PHALF, 512), F32)
        for gg in range(2):
            for q in range(4):
                sl = slot(zh * 4 + q)
                w = jnp.concatenate([wt[gg, xx, sl] for xx in range(4)], axis=1)
                acc += nt(nrm[:, pl.ds((gg * 4 + q) * 512, 512)], w)
        dst[pl.ds(pl.multiple_of(row0, PHALF), PHALF), :] = acc.astype(BF)

    prompt_kv(ozhi, tksend, 0)
    tk_copy = send(tksend, tkv.at[pl.ds(pl.multiple_of(zhi * PHALF, PHALF), PHALF), :], partner)
    got(xo)
    from_left = wo.at[g, lax.rem(x + 3, 4), pl.ds(0, 4)]
    from_right = wo.at[g, lax.rem(x + 1, 4), pl.ds(4, 4)]
    xo2 = [send(from_left, from_left, xd[1]), send(from_right, from_right, xd[3])]
    so = []
    for j in (0, 1, 3):
        piece = wo.at[g, lax.rem(x + j, 4)]
        so.append(send(piece, piece, sib))
    prompt_kv(zhi, tkv, zhi * PHALF)
    got(xo2)
    piece = wo.at[g, lax.rem(x + 2, 4)]
    so.append(send(piece, piece, sib))
    got(pg2)

    got(so)

    def attended_grad(zh, dst, row0):
        acc = jnp.zeros((HALF, FEAT), F32)
        for gg in range(2):
            for q in range(4):
                w = wo[gg, :, slot(zh * 4 + q)].reshape(4 * COLS, FEAT)
                acc += nn(pg[:, pl.ds((gg * 4 + q) * 384, 384)], w)
        dst[pl.ds(pl.multiple_of(row0, HALF), HALF), :] = acc.astype(BF)

    attended_grad(ozhi, dosend, 0)
    half_rows = pl.ds(pl.multiple_of(zhi * HALF, HALF), HALF)
    do_copy = send(dosend, dos.at[half_rows, :], partner)

    got(cnt_copies)
    total = cnts[0]
    for i in range(1, 8):
        total += cnts[i]
    live_row = total[0:1, 0:1]
    own_qkv.wait()
    got(qkv_copies)

    def keys_values(rows, src, k0, v0):
        for h in range(2):
            k = src[:, pl.ds(k0[h], 128)]
            v = src[:, pl.ds(v0[h], 128)]
            kb[h, rows, :] = k
            vb[h, rows, :] = v
            kt[h, :, rows] = k.T
            vt[h, :, rows] = v.T

    keys_values(pl.ds(0, LEN), qkvs, (128, 512), (256, 640))
    tk_copy.wait_recv()
    keys_values(pl.ds(LEN, PROMPT), tkv, (0, 256), (128, 384))

    chunks = [(c, c + KC) for c in range(0, LEN + PROMPT, KC)]

    def forward(half):
        here = pl.ds(pl.multiple_of(half * HALF, HALF), HALF)
        for h in range(2):
            q = qkvs[here, pl.ds(h * 384, 128)]
            scores, peak = [], None
            for lo, hi in chunks:
                t = nt(kb[h, lo:hi, :], q) * (score_scale * log2e)
                if lo >= LEN:
                    row = lax.broadcasted_iota(jnp.int32, t.shape, 0) + (lo - LEN)
                    t = jnp.where(row < live_row, t, masked_score)
                top = jnp.max(t, axis=0, keepdims=True)
                peak = top if peak is None else jnp.maximum(peak, top)
                scores.append(t)
            weights, norm = [], None
            for t in scores:
                e = jnp.exp2(t - peak)
                part = jnp.sum(e, axis=0, keepdims=True)
                norm = part if norm is None else norm + part
                weights.append(e)
            inv = 1.0 / norm
            o_t = None
            for (lo, hi), e in zip(chunks, weights):
                p = (e * inv).astype(BF)
                probs[h, lo:hi, here] = p
                term = nn(vt[h, :, lo:hi], p)
                o_t = term if o_t is None else o_t + term
            att[here, pl.ds(h * 128, 128)] = o_t.T.astype(BF)

    def backward(h):
        q = qkvs[:, pl.ds(h * 384, 128)]
        do = dos[:, pl.ds(h * 128, 128)]
        prod = do.astype(F32) * att[:, pl.ds(h * 128, 128)].astype(F32)
        row_dot = jnp.sum(prod.T, axis=0, keepdims=True)
        dq_t = None
        for lo, hi in chunks:
            p = probs[h, lo:hi, :]
            ds = (p.astype(F32) * (nt(vb[h, lo:hi, :], do) - row_dot)).astype(BF)
            term = nn(kt[h, :, lo:hi], ds)
            dq_t = term if dq_t is None else dq_t + term
            if hi <= LEN:
                dqs[lo:hi, pl.ds(h * 384 + 128, 128)] = (nn(ds, q) * score_scale).astype(BF)
                dqs[lo:hi, pl.ds(h * 384 + 256, 128)] = nn(p, do).astype(BF)
        dqs[:, pl.ds(h * 384, 128)] = (dq_t * score_scale).T.astype(BF)

    forward(ozhi)
    theirs = pl.ds(pl.multiple_of(ozhi * HALF, HALF), HALF)
    att_copy = send(att.at[theirs, :], aabs.at[zhi], partner)
    attended_grad(zhi, dos, zhi * HALF)
    forward(zhi)
    aabs[zhi] = att[half_rows, :]

    def turn(i, carry):
        c = pl.ds(pl.multiple_of(i * 128, 128), 128)
        pgt[c, :] = pg[:, c].T
        return carry

    lax.fori_loop(0, D // 128, turn, 0)
    do_copy.wait_recv()
    dq_copies = []

    def send_grad(h, dev, ps):
        rows = pl.ds(pl.multiple_of(ps * TOK, TOK), TOK)
        cols = pl.ds(pl.multiple_of(s * 768 + h * 384, 384), 384)
        dq_copies.append(send(dqs.at[rows, pl.ds(h * 384, 384)], dqo.at[:, cols], dev))

    for h in range(2):
        backward(h)
        if h == 0:
            att_copy.wait_recv()
        for dev, ps in reversed(clip_peers):
            send_grad(h, dev, ps)
        dqo[:, pl.ds(pl.multiple_of(s * 768 + h * 384, 384), 384)] = dqs[
            my_token_rows, pl.ds(h * 384, 384)
        ]


    def project(rows, put):
        for gg in range(2):
            for q in range(4):
                acc = None
                for zh in range(2):
                    w = wo[gg, :, slot(zh * 4 + q)].reshape(4 * COLS, FEAT)
                    term = nt(aabs[zh, rows, :], w)
                    acc = term if acc is None else acc + term
                put(pl.ds((gg * 4 + q) * 384, 384), acc)

    def project_for(j):
        def put(c, v):
            pp[j - 1, :, c] = v.astype(BF)

        project(pl.ds(pl.multiple_of(lax.rem(y + j, 4) * TOK, TOK), TOK), put)

    first, second = pl.ds(0, TOK // 2), pl.ds(TOK // 2, TOK // 2)
    def weight_grad(gg, put):
        def group(q, carry):
            rows = pl.ds(pl.multiple_of((gg * 4 + q) * 384, 384), 384)
            for zh in range(2):
                put(zh * 4 + q, nn(pgt[rows, :], aabs[zh]).reshape(4, COLS, FEAT))
            return carry

        lax.fori_loop(0, 4, group, 0)

    def put_sibling(zz, v):
        wsend[:, zz] = v.astype(BF)

    weight_grad(1 - g, put_sibling)
    w_copy = send(wsend, wrecv, sib)
    project_for(2)
    p_far = [
        send(pp.at[1, first], pa.at[0], yd[1]),
        send(pp.at[1, second], pa.at[1], yd[3]),
    ]
    project_for(1)
    p_near = [send(pp.at[0, second], pf.at[0, second], yd[1])]
    project_for(3)
    p_near.append(send(pp.at[2, first], pf.at[1, first], yd[3]))

    w_copy.wait_recv()

    def put_chip(zz, v):
        wxs[:, zz] = (v + wrecv[:, zz].astype(F32)).astype(BF)

    weight_grad(g, put_chip)
    wx_copies = [send(wxs.at[lax.rem(x + j, 4)], wxr.at[j - 1], xd[j]) for j in (2, 1, 3)]

    p_far[0].wait_recv()
    pp[0, first] = (pp[0, first].astype(F32) + pa[0].astype(F32)).astype(BF)
    p_near.append(send(pp.at[0, first], pf.at[0, first], yd[1]))
    p_far[1].wait_recv()
    pp[2, second] = (pp[2, second].astype(F32) + pa[1].astype(F32)).astype(BF)
    p_near.append(send(pp.at[2, second], pf.at[1, second], yd[3]))

    def put_own(c, v):
        pown[:, c] = v

    project(my_rows, put_own)

    got(wx_copies)

    def x_sum(i, carry):
        v = wxs[x, i].astype(F32)
        for j in range(3):
            v += wxr[j, i].astype(F32)
        wzs[i] = v.astype(BF)
        return carry

    lax.fori_loop(0, 8, x_sum, 0)
    low, high = pl.ds(0, COLS // 2), pl.ds(COLS // 2, COLS // 2)
    opposite = lax.rem(z + 4, 8)
    hop = [
        send(wzs.at[opposite, low], wz0.at[0], zd[1]),
        send(wzs.at[opposite, high], wz0.at[1], zd[7]),
    ]
    for k in range(3):
        got(hop)
        hop = []
        for way, d in ((0, 3 - k), (1, 5 + k)):
            place = lax.rem(z + d, 8)
            if k == 0:
                add = high if way else low
                wzs[place, add] = (
                    wzs[place, add].astype(F32) + wz0[way].astype(F32)
                ).astype(BF)
            else:
                wzs[place] = (wzs[place].astype(F32) + wzr[way, k - 1].astype(F32)).astype(BF)
            hop.append(send(wzs.at[place], wzr.at[way, k], zd[7 if way else 1]))

    got(p_near)
    proj = pown[...] + pf[0].astype(F32) + pf[1].astype(F32)
    bo[...] = (clip[...].astype(F32) + gate_row * proj).astype(BF)

    got(hop)
    wgo[...] = wzs[z].astype(F32) + wzr[0, 2].astype(F32) + wzr[1, 2].astype(F32)

    got(dq_copies)
    for c in started:
        c.wait_send()


def per_device(
    clip_input, qkv_input, prompt_states, prompt_ids, t5_gain, w_text, w_out, gate_table,
    timesteps, out_cotangent,
):
    gate_row = lax.dynamic_index_in_dim(gate_table, timesteps[0], 0, keepdims=True)
    vmem = pl.BlockSpec(memory_space=pltpu.VMEM)
    anym = pl.BlockSpec(memory_space=pl.ANY)
    vm = pltpu.VMEM
    scratch = [
        vm((2, 4, 8, 512, 128), BF),
        vm((2, 4, 8, COLS, FEAT), BF),
        vm((HALF, D), BF),
        vm((D, HALF), BF),
        vm((PHALF, DT), BF),
        vm((8, 8, 128), jnp.int32),
        vm((LEN, 768), BF),
        vm((LEN, FEAT), BF),
        vm((HALF, FEAT), BF),
        vm((PROMPT, 512), BF),
        vm((PHALF, 512), BF),
        vm((2, LEN + PROMPT, HD), BF),
        vm((2, LEN + PROMPT, HD), BF),
        vm((2, HD, LEN + PROMPT), BF),
        vm((2, HD, LEN + PROMPT), BF),
        vm((2, LEN + PROMPT, LEN), BF),
        vm((LEN, FEAT), BF),
        vm((2, HALF, FEAT), BF),
        vm((LEN, 768), BF),
        vm((3, TOK, D), BF),
        vm((2, TOK // 2, D), BF),
        vm((2, TOK, D), BF),
        vm((TOK, D), F32),
        vm((4, 8, COLS, FEAT), BF),
        vm((4, 8, COLS, FEAT), BF),
        vm((4, 8, COLS, FEAT), BF),
        vm((3, 8, COLS, FEAT), BF),
        vm((8, COLS, FEAT), BF),
        vm((2, COLS // 2, FEAT), BF),
        vm((2, 3, COLS, FEAT), BF),
        pltpu.SemaphoreType.DMA((N_COPIES,)),
        pltpu.SemaphoreType.DMA((N_COPIES,)),
        pltpu.SemaphoreType.DMA((1,)),
    ]
    block_out, qkv_grad, w_grad_t = pl.pallas_call(
        body,
        out_shape=(
            jax.ShapeDtypeStruct((TOK, D), BF),
            jax.ShapeDtypeStruct((TOK, H * 3 * HD), BF),
            jax.ShapeDtypeStruct((COLS, FEAT), F32),
        ),
        in_specs=[vmem] * 8 + [anym],
        out_specs=(vmem, vmem, vmem),
        scratch_shapes=scratch,
        name="block",
        cost_estimate=pl.CostEstimate(flops=12_000_000_000, bytes_accessed=10_000_000, transcendentals=3_200_000),
        compiler_params=pltpu.CompilerParams(
            collective_id=0, has_side_effects=True, vmem_limit_bytes=60 * 1024 * 1024
        ),
    )(
        gate_row, t5_gain[None], out_cotangent[0], clip_input[0], prompt_states[0], prompt_ids,
        w_text, w_out.T, qkv_input[0],
    )
    return block_out[None], qkv_grad[None], w_grad_t.T


def solution(mesh):
    in_specs = (
        P(("grp", "fsdp"), "seq", None),
        P(("grp", "fsdp"), "seq", None),
        P(("grp", "fsdp"), "seq", None),
        P(("grp", "fsdp"), "seq"),
        P(),
        P("seq", ("grp", "fsdp")),
        P("seq", ("grp", "fsdp")),
        P(),
        P(("grp", "fsdp")),
        P(("grp", "fsdp"), "seq", None),
    )
    out_specs = (
        P(("grp", "fsdp"), "seq", None),
        P(("grp", "fsdp"), "seq", None),
        P("seq", ("grp", "fsdp")),
    )
    return jax.shard_map(
        per_device, mesh=mesh, in_specs=in_specs, out_specs=out_specs, check_vma=False
    )
```

```python
import functools
import math

import jax
import jax.numpy as jnp
from jax import lax
from jax.experimental import pallas as pl
from jax.experimental.pallas import tpu as pltpu
from jax.sharding import PartitionSpec as P

H = 16
HD = 128
D = 3072
DT = 4096
LEN = 1024
PROMPT = 512
TOK = 128
PTOK = 64
HALF = 512
PHALF = 256
FEAT = 256
COLS = 96
KC = 512

MESH = pl.DeviceIdType.MESH
BF = jnp.bfloat16
F32 = jnp.float32

norm_eps = 1e-06
masked_score = -1e30
score_scale = 1.0 / math.sqrt(HD)
log2e = math.log2(math.e)

N_COPIES = 140


def nt(a, b):
    return lax.dot_general(a, b, (((1,), (1,)), ((), ())), preferred_element_type=F32)


def nn(a, b):
    return lax.dot_general(a, b, (((1,), (0,)), ((), ())), preferred_element_type=F32)


def body(
    gate, gain, cot, clip, prm, ids, wtin, woin, qkv,
    bo, dqo, wgo,
    wt, wo, pg, pgt, nrm, cnts, qkvs, dos, dosend, tkv, tksend,
    kb, vb, kt, vt, probs, att, aabs, dqs,
    pp, pa, pf, pown, wsend, wrecv, wxs, wxr, wzs, wzr,
    send_sem, recv_sem, loc_sem,
):
    g = lax.axis_index("grp")
    f = lax.axis_index("fsdp")
    s = lax.axis_index("seq")
    zlo, x = lax.div(f, 4), lax.rem(f, 4)
    zhi, y = lax.div(s, 4), lax.rem(s, 4)
    z = zhi * 4 + zlo
    ozhi = 1 - zhi

    def at(gg, xx, yy, zz):
        return (gg, lax.rem(zz, 4) * 4 + xx, lax.div(zz, 4) * 4 + yy)

    sib = at(1 - g, x, y, z)
    xd = [at(g, lax.rem(x + j, 4), y, z) for j in range(4)]
    yd = [at(g, x, lax.rem(y + j, 4), z) for j in range(4)]
    zd = [at(g, x, y, lax.rem(z + j, 8)) for j in range(8)]
    clip_peers = []
    for dz in range(2):
        for dy in range(4):
            if dz or dy:
                py, pz = lax.rem(y + dy, 4), lax.rem(z + 4 * dz, 8)
                clip_peers.append((at(g, x, py, pz), lax.div(pz, 4) * 4 + py))
    partner = zd[4]
    peers = [sib] + xd[1:] + zd[1:] + [clip_peers[i][0] for i in (0, 1, 2, 4, 5, 6)]

    barrier = pltpu.get_barrier_semaphore()
    for p in peers:
        pl.semaphore_signal(barrier, inc=1, device_id=p, device_id_type=MESH)

    started = []

    def send(src, dst, device):
        i = len(started)
        c = pltpu.make_async_remote_copy(
            src_ref=src, dst_ref=dst, send_sem=send_sem.at[i], recv_sem=recv_sem.at[i],
            device_id=device, device_id_type=MESH,
        )
        c.start()
        started.append(c)
        return c

    def slot(zz):
        d = lax.rem(zz - z + 8, 8)
        return jnp.minimum(2 * d, 15 - 2 * d)

    wo[g, x, 0] = woin[...]
    wt[g, x, 0] = wtin[...]
    pl.semaphore_wait(barrier, len(peers))

    def zstep(buf, k):
        if k < 4:
            a, b = (0, 0) if k == 1 else (2 * k - 3, 2 * k - 2)
            return [
                send(buf.at[g, x, a], buf.at[g, x, 2 * k - 1], zd[1]),
                send(buf.at[g, x, b], buf.at[g, x, 2 * k], zd[7]),
            ]
        h = buf.shape[3] // 2
        top, bottom = pl.ds(0, h), pl.ds(h, h)
        return [
            send(buf.at[g, x, 5, top], buf.at[g, x, 7, top], zd[1]),
            send(buf.at[g, x, 6, bottom], buf.at[g, x, 7, bottom], zd[7]),
        ]

    groups = ((0, 1), (1, 2), (3, 2), (5, 2), (7, 1))

    def xfirst(buf, k):
        sl = pl.ds(*groups[k])
        mine = buf.at[g, x, sl]
        return [send(mine, mine, xd[1]), send(mine, mine, xd[3])]

    def xsecond(buf, k):
        first, n = groups[k]
        lx, rx = lax.rem(x + 3, 4), lax.rem(x + 1, 4)
        if n == 2:
            from_left, from_right = buf.at[g, lx, first], buf.at[g, rx, first + 1]
        else:
            h = buf.shape[3] // 2
            from_left = buf.at[g, lx, first, pl.ds(0, h)]
            from_right = buf.at[g, rx, first, pl.ds(h, h)]
        return [send(from_left, from_left, xd[1]), send(from_right, from_right, xd[3])]

    def to_sibling(buf, k):
        both = buf.at[g, :, pl.ds(*groups[k])]
        return [send(both, both, sib)]

    def got(copies):
        for c in copies:
            c.wait_recv()

    def yfirst(buf, n):
        mine = buf.at[pl.ds(pl.multiple_of(y * n, n), n), :]
        return [send(mine, mine, yd[1]), send(mine, mine, yd[3])]

    def ysecond(buf, n):
        h = n // 2
        from_left = buf.at[pl.ds(pl.multiple_of(lax.rem(y + 3, 4) * n, n), h), :]
        from_right = buf.at[pl.ds(pl.multiple_of(lax.rem(y + 1, 4) * n + h, h), h), :]
        return [send(from_left, from_left, yd[1]), send(from_right, from_right, yd[3])]

    zt, zo, xt, xt2, st = {}, {}, {}, {}, {}
    qkv_copies = []

    def send_qkv(peer, part=0, parts=1):
        dev, ps = clip_peers[peer]
        n = TOK // parts
        qkv_copies.append(
            send(
                qkv.at[pl.ds(part * n, n), pl.ds(pl.multiple_of(ps * 768, 768), 768)],
                qkvs.at[pl.ds(pl.multiple_of(s * TOK + part * n, n), n), :],
                dev,
            )
        )

    zt[1] = zstep(wt, 1)
    xt[0] = xfirst(wt, 0)
    zo[1] = zstep(wo, 1)
    send_qkv(3, 0, 4)
    my_prompt = pl.ds(pl.multiple_of(y * PTOK, PTOK), PTOK)
    wide = prm[...].astype(F32)
    mean = jnp.mean(wide * wide, axis=-1, keepdims=True)
    nrm[my_prompt, :] = (wide * lax.rsqrt(mean + norm_eps) * gain[...]).astype(BF)
    n1 = yfirst(nrm, PTOK)
    gate_row = gate[...].astype(F32)
    my_rows = pl.ds(pl.multiple_of(y * TOK, TOK), TOK)
    pg[my_rows, :] = (gate_row * cot[...].astype(F32)).astype(BF)
    live = jnp.sum((ids[...] != 0).astype(jnp.int32), axis=-1, keepdims=True)
    cnts[0] = jnp.broadcast_to(live, (8, 128))
    cnt_copies = [
        send(cnts.at[0], cnts.at[i + 1], dev) for i, (dev, _) in enumerate(clip_peers)
    ]
    my_token_rows = pl.ds(pl.multiple_of(s * TOK, TOK), TOK)
    own_qkv = pltpu.make_async_copy(
        qkv.at[:, pl.ds(pl.multiple_of(s * 768, 768), 768)], qkvs.at[my_token_rows, :], loc_sem.at[0]
    )
    own_qkv.start()

    for k in range(1, 5):
        got(zt[k])
        if k < 4:
            zt[k + 1] = zstep(wt, k + 1)
        xt[k] = xfirst(wt, k)
        got(zo[k])
        if k < 4:
            zo[k + 1] = zstep(wo, k + 1)
            send_qkv(3, k, 4)
        else:
            for peer in (6, 5, 4):
                send_qkv(peer)
        if k == 2:
            got(n1)
            n2 = ysecond(nrm, PTOK)
            pg1 = yfirst(pg, TOK)
        got(xt[k - 1])
        xt2[k - 1] = xsecond(wt, k - 1)
        if k >= 2:
            got(xt2[k - 2])
            st[k - 2] = to_sibling(wt, k - 2)
    got(pg1)
    pg2 = ysecond(pg, TOK)
    for peer in (2, 1, 0):
        send_qkv(peer)
    got(xt[4])
    xt2[4] = xsecond(wt, 4)
    mine = wo.at[g, x]
    xo = [send(mine, mine, xd[1]), send(mine, mine, xd[3])]
    got(xt2[3])
    st[3] = to_sibling(wt, 3)
    got(xt2[4])
    st[4] = to_sibling(wt, 4)
    got(n2)
    for k in range(5):
        got(st[k])

    def prompt_kv(zh, dst, row0):
        acc = jnp.zeros((PHALF, 512), F32)
        for gg in range(2):
            for q in range(4):
                sl = slot(zh * 4 + q)
                w = jnp.concatenate([wt[gg, xx, sl] for xx in range(4)], axis=1)
                acc += nt(nrm[:, pl.ds((gg * 4 + q) * 512, 512)], w)
        dst[pl.ds(pl.multiple_of(row0, PHALF), PHALF), :] = acc.astype(BF)

    prompt_kv(ozhi, tksend, 0)
    tk_copy = send(tksend, tkv.at[pl.ds(pl.multiple_of(zhi * PHALF, PHALF), PHALF), :], partner)
    got(xo)
    from_left = wo.at[g, lax.rem(x + 3, 4), pl.ds(0, 4)]
    from_right = wo.at[g, lax.rem(x + 1, 4), pl.ds(4, 4)]
    xo2 = [send(from_left, from_left, xd[1]), send(from_right, from_right, xd[3])]
    so = []
    for j in (0, 1, 3):
        piece = wo.at[g, lax.rem(x + j, 4)]
        so.append(send(piece, piece, sib))
    prompt_kv(zhi, tkv, zhi * PHALF)
    got(xo2)
    piece = wo.at[g, lax.rem(x + 2, 4)]
    so.append(send(piece, piece, sib))
    got(pg2)

    got(so)

    def attended_grad(zh, dst, row0):
        acc = jnp.zeros((HALF, FEAT), F32)
        for gg in range(2):
            for q in range(4):
                w = wo[gg, :, slot(zh * 4 + q)].reshape(4 * COLS, FEAT)
                acc += nn(pg[:, pl.ds((gg * 4 + q) * 384, 384)], w)
        dst[pl.ds(pl.multiple_of(row0, HALF), HALF), :] = acc.astype(BF)

    attended_grad(ozhi, dosend, 0)
    half_rows = pl.ds(pl.multiple_of(zhi * HALF, HALF), HALF)
    do_copy = send(dosend, dos.at[half_rows, :], partner)

    got(cnt_copies)
    total = cnts[0]
    for i in range(1, 8):
        total += cnts[i]
    live_row = total[0:1, 0:1]
    own_qkv.wait()
    got(qkv_copies)

    def keys_values(rows, src, k0, v0):
        for h in range(2):
            k = src[:, pl.ds(k0[h], 128)]
            v = src[:, pl.ds(v0[h], 128)]
            kb[h, rows, :] = k
            vb[h, rows, :] = v
            kt[h, :, rows] = k.T
            vt[h, :, rows] = v.T

    keys_values(pl.ds(0, LEN), qkvs, (128, 512), (256, 640))
    tk_copy.wait_recv()
    keys_values(pl.ds(LEN, PROMPT), tkv, (0, 256), (128, 384))

    chunks = [(c, c + KC) for c in range(0, LEN + PROMPT, KC)]

    def forward(half):
        here = pl.ds(pl.multiple_of(half * HALF, HALF), HALF)
        for h in range(2):
            q = qkvs[here, pl.ds(h * 384, 128)]
            scores, peak = [], None
            for lo, hi in chunks:
                t = nt(kb[h, lo:hi, :], q) * (score_scale * log2e)
                if lo >= LEN:
                    row = lax.broadcasted_iota(jnp.int32, t.shape, 0) + (lo - LEN)
                    t = jnp.where(row < live_row, t, masked_score)
                top = jnp.max(t, axis=0, keepdims=True)
                peak = top if peak is None else jnp.maximum(peak, top)
                scores.append(t)
            weights, norm = [], None
            for t in scores:
                e = jnp.exp2(t - peak)
                part = jnp.sum(e, axis=0, keepdims=True)
                norm = part if norm is None else norm + part
                weights.append(e)
            inv = 1.0 / norm
            o_t = None
            for (lo, hi), e in zip(chunks, weights):
                p = (e * inv).astype(BF)
                probs[h, lo:hi, here] = p
                term = nn(vt[h, :, lo:hi], p)
                o_t = term if o_t is None else o_t + term
            att[here, pl.ds(h * 128, 128)] = o_t.T.astype(BF)

    def backward(h):
        q = qkvs[:, pl.ds(h * 384, 128)]
        do = dos[:, pl.ds(h * 128, 128)]
        prod = do.astype(F32) * att[:, pl.ds(h * 128, 128)].astype(F32)
        row_dot = jnp.sum(prod.T, axis=0, keepdims=True)
        dq_t = None
        for lo, hi in chunks:
            p = probs[h, lo:hi, :]
            ds = (p.astype(F32) * (nt(vb[h, lo:hi, :], do) - row_dot)).astype(BF)
            term = nn(kt[h, :, lo:hi], ds)
            dq_t = term if dq_t is None else dq_t + term
            if hi <= LEN:
                dqs[lo:hi, pl.ds(h * 384 + 128, 128)] = (nn(ds, q) * score_scale).astype(BF)
                dqs[lo:hi, pl.ds(h * 384 + 256, 128)] = nn(p, do).astype(BF)
        dqs[:, pl.ds(h * 384, 128)] = (dq_t * score_scale).T.astype(BF)

    forward(ozhi)
    theirs = pl.ds(pl.multiple_of(ozhi * HALF, HALF), HALF)
    att_copy = send(att.at[theirs, :], aabs.at[zhi], partner)
    attended_grad(zhi, dos, zhi * HALF)
    forward(zhi)
    aabs[zhi] = att[half_rows, :]

    def turn(i, carry):
        c = pl.ds(pl.multiple_of(i * 128, 128), 128)
        pgt[c, :] = pg[:, c].T
        return carry

    lax.fori_loop(0, D // 128, turn, 0)
    do_copy.wait_recv()
    dq_copies = []

    def send_grad(h, dev, ps):
        rows = pl.ds(pl.multiple_of(ps * TOK, TOK), TOK)
        cols = pl.ds(pl.multiple_of(s * 768 + h * 384, 384), 384)
        dq_copies.append(send(dqs.at[rows, pl.ds(h * 384, 384)], dqo.at[:, cols], dev))

    for h in range(2):
        backward(h)
        if h == 0:
            att_copy.wait_recv()
        for dev, ps in reversed(clip_peers):
            send_grad(h, dev, ps)
        dqo[:, pl.ds(pl.multiple_of(s * 768 + h * 384, 384), 384)] = dqs[
            my_token_rows, pl.ds(h * 384, 384)
        ]


    def project(rows, put):
        for gg in range(2):
            for q in range(4):
                acc = None
                for zh in range(2):
                    w = wo[gg, :, slot(zh * 4 + q)].reshape(4 * COLS, FEAT)
                    term = nt(aabs[zh, rows, :], w)
                    acc = term if acc is None else acc + term
                put(pl.ds((gg * 4 + q) * 384, 384), acc)

    def project_for(j):
        def put(c, v):
            pp[j - 1, :, c] = v.astype(BF)

        project(pl.ds(pl.multiple_of(lax.rem(y + j, 4) * TOK, TOK), TOK), put)

    first, second = pl.ds(0, TOK // 2), pl.ds(TOK // 2, TOK // 2)
    def weight_grad(gg, put):
        def group(q, carry):
            rows = pl.ds(pl.multiple_of((gg * 4 + q) * 384, 384), 384)
            for zh in range(2):
                put(zh * 4 + q, nn(pgt[rows, :], aabs[zh]).reshape(4, COLS, FEAT))
            return carry

        lax.fori_loop(0, 4, group, 0)

    def put_sibling(zz, v):
        wsend[:, zz] = v.astype(BF)

    weight_grad(1 - g, put_sibling)
    w_copy = send(wsend, wrecv, sib)
    project_for(2)
    p_far = [
        send(pp.at[1, first], pa.at[0], yd[1]),
        send(pp.at[1, second], pa.at[1], yd[3]),
    ]
    project_for(1)
    p_near = [send(pp.at[0, second], pf.at[0, second], yd[1])]
    project_for(3)
    p_near.append(send(pp.at[2, first], pf.at[1, first], yd[3]))

    w_copy.wait_recv()

    def put_chip(zz, v):
        wxs[:, zz] = (v + wrecv[:, zz].astype(F32)).astype(BF)

    weight_grad(g, put_chip)
    wx_copies = [send(wxs.at[lax.rem(x + j, 4)], wxr.at[j - 1], xd[j]) for j in (2, 1, 3)]

    p_far[0].wait_recv()
    pp[0, first] = (pp[0, first].astype(F32) + pa[0].astype(F32)).astype(BF)
    p_near.append(send(pp.at[0, first], pf.at[0, first], yd[1]))
    p_far[1].wait_recv()
    pp[2, second] = (pp[2, second].astype(F32) + pa[1].astype(F32)).astype(BF)
    p_near.append(send(pp.at[2, second], pf.at[1, second], yd[3]))

    def put_own(c, v):
        pown[:, c] = v

    project(my_rows, put_own)

    got(wx_copies)

    def x_sum(i, carry):
        v = wxs[x, i].astype(F32)
        for j in range(3):
            v += wxr[j, i].astype(F32)
        wzs[i] = v.astype(BF)
        return carry

    lax.fori_loop(0, 8, x_sum, 0)
    wz_copies = [send(wzs.at[lax.rem(z + j, 8)], wzr.at[j - 1], zd[j]) for j in (4, 3, 5, 2, 6, 1, 7)]

    got(p_near)
    proj = pown[...] + pf[0].astype(F32) + pf[1].astype(F32)
    bo[...] = (clip[...].astype(F32) + gate_row * proj).astype(BF)

    got(wz_copies)
    v = wzs[z].astype(F32)
    for j in range(7):
        v += wzr[j].astype(F32)
    wgo[...] = v

    got(dq_copies)
    for c in started:
        c.wait_send()


def per_device(
    clip_input, qkv_input, prompt_states, prompt_ids, t5_gain, w_text, w_out, gate_table,
    timesteps, out_cotangent,
):
    gate_row = lax.dynamic_index_in_dim(gate_table, timesteps[0], 0, keepdims=True)
    vmem = pl.BlockSpec(memory_space=pltpu.VMEM)
    anym = pl.BlockSpec(memory_space=pl.ANY)
    vm = pltpu.VMEM
    scratch = [
        vm((2, 4, 8, 512, 128), BF),
        vm((2, 4, 8, COLS, FEAT), BF),
        vm((HALF, D), BF),
        vm((D, HALF), BF),
        vm((PHALF, DT), BF),
        vm((8, 8, 128), jnp.int32),
        vm((LEN, 768), BF),
        vm((LEN, FEAT), BF),
        vm((HALF, FEAT), BF),
        vm((PROMPT, 512), BF),
        vm((PHALF, 512), BF),
        vm((2, LEN + PROMPT, HD), BF),
        vm((2, LEN + PROMPT, HD), BF),
        vm((2, HD, LEN + PROMPT), BF),
        vm((2, HD, LEN + PROMPT), BF),
        vm((2, LEN + PROMPT, LEN), BF),
        vm((LEN, FEAT), BF),
        vm((2, HALF, FEAT), BF),
        vm((LEN, 768), BF),
        vm((3, TOK, D), BF),
        vm((2, TOK // 2, D), BF),
        vm((2, TOK, D), BF),
        vm((TOK, D), F32),
        vm((4, 8, COLS, FEAT), BF),
        vm((4, 8, COLS, FEAT), BF),
        vm((4, 8, COLS, FEAT), BF),
        vm((3, 8, COLS, FEAT), BF),
        vm((8, COLS, FEAT), BF),
        vm((7, COLS, FEAT), BF),
        pltpu.SemaphoreType.DMA((N_COPIES,)),
        pltpu.SemaphoreType.DMA((N_COPIES,)),
        pltpu.SemaphoreType.DMA((1,)),
    ]
    block_out, qkv_grad, w_grad_t = pl.pallas_call(
        body,
        out_shape=(
            jax.ShapeDtypeStruct((TOK, D), BF),
            jax.ShapeDtypeStruct((TOK, H * 3 * HD), BF),
            jax.ShapeDtypeStruct((COLS, FEAT), F32),
        ),
        in_specs=[vmem] * 8 + [anym],
        out_specs=(vmem, vmem, vmem),
        scratch_shapes=scratch,
        name="block",
        cost_estimate=pl.CostEstimate(flops=12_000_000_000, bytes_accessed=10_000_000, transcendentals=3_200_000),
        compiler_params=pltpu.CompilerParams(
            collective_id=0, has_side_effects=True, vmem_limit_bytes=60 * 1024 * 1024
        ),
    )(
        gate_row, t5_gain[None], out_cotangent[0], clip_input[0], prompt_states[0], prompt_ids,
        w_text, w_out.T, qkv_input[0],
    )
    return block_out[None], qkv_grad[None], w_grad_t.T


def solution(mesh):
    in_specs = (
        P(("grp", "fsdp"), "seq", None),
        P(("grp", "fsdp"), "seq", None),
        P(("grp", "fsdp"), "seq", None),
        P(("grp", "fsdp"), "seq"),
        P(),
        P("seq", ("grp", "fsdp")),
        P("seq", ("grp", "fsdp")),
        P(),
        P(("grp", "fsdp")),
        P(("grp", "fsdp"), "seq", None),
    )
    out_specs = (
        P(("grp", "fsdp"), "seq", None),
        P(("grp", "fsdp"), "seq", None),
        P("seq", ("grp", "fsdp")),
    )
    return jax.shard_map(
        per_device, mesh=mesh, in_specs=in_specs, out_specs=out_specs, check_vma=False
    )
```
